512 devices in a mesh: dp: 64 (over z, x, core), tensor: 8 (over y).
Axes of the slice: x: 4, y: 8, z: 8, core: 2. Of those that a mesh axis runs over, the one named last changes fastest.
Arguments:
- gradient: bfloat16 [512, 53248], P('dp', 'tensor'), may hold values from -1.5 to 1.5
- block_list: int32 [64, 2], P('dp'), may hold values from 0 to 51, as said below
- block_counts: int32 [64], P('dp'), may hold values from 0 to 2, as said below
- stats: float32 [64, 2, 1024, 1024], P('dp', None, None, 'tensor'), as said below
- basis: bfloat16 [64, 2, 1024, 1024], P('dp', None, None, 'tensor'), may hold values from -0.1875 to 0.1875
- first_moment: float32 [64, 2, 512, 1024], P('dp', None, None, 'tensor'), may hold values from -2 to 2
- second_moment: float32 [64, 2, 512, 1024], P('dp', None, None, 'tensor'), may hold values from 0.01 to 1
Outputs:
- update: bfloat16 [512, 53248], P('dp', 'tensor')
- new_stats: float32 [64, 2, 1024, 1024], P('dp', None, None, 'tensor')
- new_first: float32 [64, 2, 512, 1024], P('dp', None, None, 'tensor')
- new_second: float32 [64, 2, 512, 1024], P('dp', None, None, 'tensor')
The draws below stay inside these ranges and needn't reach their ends.
Inputs may be any that keep to these rules, and one draw needn't show every extreme that they name: `block_list`: the first block_counts[o] entries of row o name the blocks that owner o updates; over all owners these name every one of the 52 blocks exactly once. Later entries are ignored. `block_counts`: they sum to 52; some owner holds exactly 2 blocks. `stats`: Symmetric.
All inputs are finite; a program needn't handle non-finite values.
Results may differ from the reference program's by a relative error of at most 0.0049.
Values may be sent and summed in bfloat16 or wider, within the bound.
No kernel may reach another device: no remote copies, remote signals or barrier semaphores. Data moves between devices by JAX's collectives and lax.ppermute only.
A program may use at most 64 MiB of HBM per device.

```python
import math
import jax
import jax.numpy as jnp
from jax import lax

FF = 53248
BW = 1024
STEP = 10
ROWS = 512
BLOCKS = 52
SLOTS = 2
N_DP = 64


def owner_layout(key):
    total = N_DP * SLOTS
    busiest = jax.random.randint(jax.random.fold_in(key, 11), (), 0, N_DP)
    scores = jax.random.permutation(jax.random.fold_in(key, 12), total).reshape(N_DP, SLOTS)
    owner_ids = jnp.arange(N_DP)[:, None]
    scores = jnp.where(owner_ids == busiest, scores - total, scores).reshape(-1)
    ranking = jnp.argsort(jnp.argsort(scores))
    chosen = (ranking < BLOCKS).reshape(N_DP, SLOTS)
    counts = jnp.sum(chosen.astype(jnp.int32), axis=1)
    live_slots = jnp.arange(SLOTS)[None, :] < counts[:, None]
    position = jnp.cumsum(live_slots.reshape(-1).astype(jnp.int32)) - 1
    shuffled = jax.random.permutation(jax.random.fold_in(key, 13), BLOCKS)
    named = shuffled[jnp.clip(position, 0, BLOCKS - 1)].reshape(N_DP, SLOTS)
    filler = jax.random.randint(jax.random.fold_in(key, 14), (N_DP, SLOTS), 0, BLOCKS)
    return (jnp.where(live_slots, named, filler).astype(jnp.int32), counts.astype(jnp.int32))


def draw_block_list(key, part):
    return owner_layout(key)[0]


def draw_block_counts(key, part):
    return owner_layout(key)[1]


def draw_stats(key, part):
    key = jax.random.fold_in(key, 3)
    shape = (N_DP, SLOTS, BW, BW)
    noise = jax.random.normal(key, shape, jnp.float32)
    identity = jnp.eye(BW, dtype=jnp.float32)
    return (noise + jnp.swapaxes(noise, -1, -2) + 4.0 * identity).astype(jnp.float32)


def block_scale(stream_key, dims, shards, low, top_value):
    def one(dim, blocks):
        steps = jax.random.uniform(jax.random.fold_in(jax.random.fold_in(stream_key, 6), dim), (blocks,), jnp.float32, low / len(shards), top_value / len(shards))
        return jnp.repeat(jnp.exp(steps), dims[dim] // blocks).reshape((-1,) + (1,) * (len(dims) - dim - 1))

    gain = one(*shards[0])
    for cut in shards[1:]:
        gain = gain * one(*cut)
    return gain


def gaussian(rng, extent, scale, reach, pieces=(), kind=jnp.bfloat16):
    level = block_scale(rng, extent, pieces, -0.22, 0.18) if pieces else 1.0
    drawn = jax.random.normal(rng, extent, jnp.float32) * scale * level
    return jnp.minimum(jnp.maximum(drawn, -reach), reach).astype(kind)


def setup_inputs(seed: int = 0) -> dict:
    seeds = jax.random.split(jax.random.key(seed), 8)
    gradient = gaussian(seeds[0], (ROWS, FF), 0.25, 1.5, ((0, 64), (1, 8)))
    block_list = draw_block_list(jax.random.fold_in(seeds[7], 71), 0)
    block_counts = draw_block_counts(jax.random.fold_in(seeds[7], 71), 0)
    stats = draw_stats(jax.random.fold_in(seeds[7], 71), 0)
    basis = gaussian(seeds[4], (N_DP, SLOTS, BW, BW), BW ** -0.5, 0.1875, ((0, 64), (3, 8)))
    first_moment = gaussian(seeds[5], (N_DP, SLOTS, ROWS, BW), 0.3, 2.0, ((0, 64), (3, 8)), jnp.float32)
    second_moment = jnp.clip(jnp.exp(math.log(1.0) - 4.6051702 * jax.random.uniform(seeds[6], (N_DP, SLOTS, ROWS, BW), jnp.float32) ** block_scale(seeds[6], (N_DP, SLOTS, ROWS, BW), ((0, 64), (3, 8)), -0.2, 0.2)), 0.01, 1.0)
    return dict(gradient=gradient, block_list=block_list, block_counts=block_counts, stats=stats, basis=basis, first_moment=first_moment, second_moment=second_moment)


beta_one = 0.9
beta_two = 0.95
beta_stat = 0.95
epsilon = 1e-08

def reference(gradient, block_list, block_counts, stats, basis, first_moment, second_moment):
    total = N_DP * SLOTS
    by_block = gradient.reshape(ROWS, BLOCKS, BW).transpose(1, 0, 2)
    flat_lists = block_list.reshape(-1)
    live_flat = (jnp.arange(SLOTS)[None, :] < block_counts[:, None]).reshape(-1)
    stats_flat = stats.reshape(total, BW, BW)
    basis_flat = basis.reshape(total, BW, BW)
    first_flat = first_moment.reshape(total, ROWS, BW)
    second_flat = second_moment.reshape(total, ROWS, BW)
    bias_one = 1.0 - beta_one ** STEP
    bias_two = 1.0 - beta_two ** STEP

    def per_slot(slot_index):
        block_grad = by_block[flat_lists[slot_index]]
        rotation = basis_flat[slot_index]
        rotated = jnp.dot(block_grad, rotation, preferred_element_type=jnp.float32)
        moment_one = beta_one * first_flat[slot_index] + (1.0 - beta_one) * rotated
        moment_two = beta_two * second_flat[slot_index] + (1.0 - beta_two) * rotated * rotated
        direction = (moment_one / bias_one / (jnp.sqrt(moment_two / bias_two) + epsilon)).astype(jnp.bfloat16)
        updates = jnp.dot(direction, rotation.T, preferred_element_type=jnp.float32).astype(jnp.bfloat16)
        gram_part = jnp.dot(block_grad.T, block_grad, preferred_element_type=jnp.float32)
        new_stat = beta_stat * stats_flat[slot_index] + (1.0 - beta_stat) * gram_part
        is_live = live_flat[slot_index]
        return (jnp.where(is_live, new_stat, stats_flat[slot_index]), jnp.where(is_live, moment_one, first_flat[slot_index]), jnp.where(is_live, moment_two, second_flat[slot_index]), updates)
    new_stat, new_one, new_two, updates = lax.map(per_slot, jnp.arange(total))
    matches = ((flat_lists[None, :] == jnp.arange(BLOCKS)[:, None]) & live_flat[None, :]).astype(jnp.float32)
    placed = jnp.dot(matches, updates.astype(jnp.float32).reshape(total, ROWS * BW), preferred_element_type=jnp.float32)
    update = placed.reshape(BLOCKS, ROWS, BW).transpose(1, 0, 2).reshape(ROWS, FF).astype(jnp.bfloat16)
    return (update, new_stat.reshape(stats.shape), new_one.reshape(first_moment.shape), new_two.reshape(second_moment.shape))
```

```python
import jax
import jax.numpy as jnp
from jax import lax
from jax.experimental import pallas as pl
from jax.experimental.pallas import tpu as pltpu
from jax.sharding import PartitionSpec as P

STEP = 10


beta_one = 0.9
beta_two = 0.95
beta_stat = 0.95
epsilon = 1e-08
bias_one = 1.0 - beta_one**STEP
bias_two = 1.0 - beta_two**STEP


def rows_kernel(grad_ref, basis_ref, first_ref, second_ref, rotated_ref, back_ref):
    parts, slots = basis_ref.shape[:2]
    for s in range(slots):
        grad = grad_ref[s]
        total = None
        for k in range(parts):
            basis = basis_ref[k, s]
            rotated = jnp.dot(grad, basis, preferred_element_type=jnp.float32)
            rotated_ref[k, s] = rotated
            moment_one = beta_one * first_ref[k, s] + (1.0 - beta_one) * rotated
            moment_two = (
                beta_two * second_ref[k, s].astype(jnp.float32) + (1.0 - beta_two) * rotated * rotated
            )
            direction = (
                moment_one / bias_one / (jnp.sqrt(moment_two / bias_two) + epsilon)
            ).astype(jnp.bfloat16)
            term = lax.dot_general(
                direction, basis, (((1,), (1,)), ((), ())), preferred_element_type=jnp.float32
            )
            total = term if total is None else total + term
        back_ref[s] = total.astype(back_ref.dtype)


def on_device(gradient, block_list, block_counts, stats, basis, first_moment, second_moment):
    rows_dev, cols_dev = gradient.shape
    slot_count = block_list.shape[1]
    owners = lax.axis_size("dp")
    parts = lax.axis_size("tensor")
    width = stats.shape[2]
    part = stats.shape[3]
    blocks = cols_dev * parts // width

    mine = jnp.concatenate([block_list, block_counts[:, None]], axis=1)
    table = lax.all_to_all(
        jnp.broadcast_to(mine, (owners, slot_count + 1)), "dp", 0, 0, tiled=True
    )
    lists = table[:, :slot_count]
    live = jnp.arange(slot_count)[None, :] < table[:, slot_count:]

    basis_all = lax.all_gather(basis[0], "tensor", axis=0, tiled=False)

    def to_rows(x):
        y = x.reshape(slot_count, owners, parts, part).transpose(2, 0, 1, 3)
        return lax.all_to_all(y, "tensor", 0, 0, tiled=True)

    first_rows = to_rows(first_moment[0])
    second_rows = to_rows(second_moment[0])

    row = lax.all_to_all(
        gradient.reshape(rows_dev, cols_dev // part, part), "tensor", 0, 0, tiled=True
    )
    by_block = row.reshape(blocks, width // part, part)
    outgoing = jnp.take(by_block, lists, axis=0, mode="clip")
    arrived = lax.all_to_all(outgoing, "dp", 0, 0, tiled=True)
    grad_rows = arrived.transpose(1, 0, 2, 3).reshape(slot_count, owners, width)

    rotated, back = pl.pallas_call(
        rows_kernel,
        out_shape=(
            jax.ShapeDtypeStruct(first_rows.shape, jnp.float32),
            jax.ShapeDtypeStruct(grad_rows.shape, jnp.bfloat16),
        ),
        compiler_params=pltpu.CompilerParams(vmem_limit_bytes=48 * 2**20),
        name="rotate_rows",
    )(grad_rows, basis_all, first_rows, second_rows)

    back_out = back.reshape(slot_count, owners, width // part, part).transpose(1, 0, 2, 3)
    returned = lax.all_to_all(back_out, "dp", 0, 0, tiled=True)
    holds = (lists.reshape(-1)[None, :] == jnp.arange(blocks)[:, None]) & live.reshape(-1)[None, :]
    place = jnp.argmax(holds, axis=1)
    placed = jnp.take(
        returned.reshape(owners * slot_count, width // part, part), place, axis=0, mode="clip"
    )
    update = lax.all_to_all(
        placed.reshape(parts, cols_dev // part, part), "tensor", 0, 0, tiled=True
    ).reshape(rows_dev, cols_dev)

    live_here = (jnp.arange(slot_count) < block_counts[0])[:, None, None]
    rotated_cols = (
        lax.all_to_all(rotated, "tensor", 0, 0, tiled=True)
        .transpose(1, 2, 0, 3)
        .reshape(slot_count, owners * parts, part)
    )
    moment_one = beta_one * first_moment[0] + (1.0 - beta_one) * rotated_cols
    moment_two = beta_two * second_moment[0] + (1.0 - beta_two) * rotated_cols * rotated_cols
    grad_all = lax.all_gather(grad_rows, "tensor", axis=1, tiled=True)
    grad_cols = lax.dynamic_slice_in_dim(grad_all, lax.axis_index("tensor") * part, part, 2)
    gram = jnp.einsum("srb,src->sbc", grad_all, grad_cols, preferred_element_type=jnp.float32)
    new_stat = beta_stat * stats[0] + (1.0 - beta_stat) * gram
    new_stats = jnp.where(live_here, new_stat, stats[0])[None]
    new_first = jnp.where(live_here, moment_one, first_moment[0])[None]
    new_second = jnp.where(live_here, moment_two, second_moment[0])[None]
    return (update, new_stats, new_first, new_second)


def solution(mesh):
    placed = (
        P("dp", "tensor"),
        P("dp", None),
        P("dp"),
        P("dp", None, None, "tensor"),
        P("dp", None, None, "tensor"),
        P("dp", None, None, "tensor"),
        P("dp", None, None, "tensor"),
    )
    return jax.shard_map(
        on_device,
        mesh=mesh,
        in_specs=placed,
        out_specs=(
            P("dp", "tensor"),
            P("dp", None, None, "tensor"),
            P("dp", None, None, "tensor"),
            P("dp", None, None, "tensor"),
        ),
        check_vma=False,
    )
```

```python
import jax
import jax.numpy as jnp
from jax import lax
from jax.experimental import pallas as pl
from jax.experimental.pallas import tpu as pltpu
from jax.sharding import PartitionSpec as P

STEP = 10


beta_one = 0.9
beta_two = 0.95
beta_stat = 0.95
epsilon = 1e-08
bias_one = 1.0 - beta_one**STEP
bias_two = 1.0 - beta_two**STEP


def rows_kernel(grad_ref, basis_ref, moved_ref, back_ref):
    parts, slots = basis_ref.shape[:2]
    rows = grad_ref.shape[1]
    for s in range(slots):
        grad = grad_ref[s]
        total = None
        for k in range(parts):
            basis = basis_ref[k, s]
            rotated = jnp.dot(grad, basis, preferred_element_type=jnp.float32)
            first_high, first_low, second = (
                moved_ref[k, pl.ds((i * slots + s) * rows, rows), :].astype(jnp.float32)
                for i in range(3)
            )
            moment_one = beta_one * (first_high + first_low) + (1.0 - beta_one) * rotated
            moment_two = beta_two * second + (1.0 - beta_two) * rotated * rotated
            direction = (
                moment_one / bias_one / (jnp.sqrt(moment_two / bias_two) + epsilon)
            ).astype(jnp.bfloat16)
            term = lax.dot_general(
                direction, basis, (((1,), (1,)), ((), ())), preferred_element_type=jnp.float32
            )
            total = term if total is None else total + term
        back_ref[s] = total.astype(back_ref.dtype)


def state_kernel(
    count_ref, grad_ref, basis_ref, stats_ref, first_ref, second_ref,
    new_stats_ref, new_first_ref, new_second_ref,
):
    parts, slots, rows, width = grad_ref.shape
    part = basis_ref.shape[2]
    start = pl.multiple_of(lax.axis_index("tensor") * part, part)
    for s in range(slots):
        live = s < count_ref[0]
        grad = grad_ref[:, s].reshape(parts * rows, width)
        grad_cols = grad_ref[:, s, :, pl.ds(start, part)].reshape(parts * rows, part)
        gram = lax.dot_general(
            grad, grad_cols, (((0,), (0,)), ((), ())), preferred_element_type=jnp.float32
        )
        stats = stats_ref[s]
        new_stats_ref[s] = jnp.where(live, beta_stat * stats + (1.0 - beta_stat) * gram, stats)
        rotated_all = jnp.dot(grad, basis_ref[s], preferred_element_type=jnp.float32)
        for t in range(parts):
            rotated = rotated_all[t * rows : (t + 1) * rows]
            here = pl.ds(t, rows, stride=parts)
            first = first_ref[s, here, :]
            second = second_ref[s, here, :]
            new_first_ref[s, here, :] = jnp.where(
                live, beta_one * first + (1.0 - beta_one) * rotated, first
            )
            new_second_ref[s, here, :] = jnp.where(
                live, beta_two * second + (1.0 - beta_two) * rotated * rotated, second
            )


def on_device(gradient, block_list, block_counts, stats, basis, first_moment, second_moment):
    rows_dev, cols_dev = gradient.shape
    slot_count = block_list.shape[1]
    owners = lax.axis_size("dp")
    parts = lax.axis_size("tensor")
    width = stats.shape[2]
    part = stats.shape[3]
    blocks = cols_dev * parts // width

    basis_all = lax.all_gather(basis[0], "tensor", axis=0, tiled=False)

    mine = jnp.concatenate([block_list[0], block_counts])
    is_me = jnp.arange(owners)[:, None] == lax.axis_index("dp")
    table = lax.psum(jnp.where(is_me, mine[None, :], 0), "dp")
    lists = table[:, :slot_count]
    live = jnp.arange(slot_count)[None, :] < table[:, slot_count:]

    def rows_of(x):
        return x.reshape(slot_count, owners, parts, part).transpose(2, 0, 1, 3).reshape(
            parts, slot_count * owners, part
        )

    first = rows_of(first_moment[0])
    first_high = first.astype(jnp.bfloat16)
    first_low = (first - first_high.astype(jnp.float32)).astype(jnp.bfloat16)
    second_high = rows_of(second_moment[0]).astype(jnp.bfloat16)
    sent = jnp.concatenate(
        [first_high, first_low, second_high, gradient.reshape(rows_dev, cols_dev // part, part)],
        axis=1,
    )
    moved = lax.all_to_all(sent, "tensor", 0, 0, tiled=True)
    by_block = moved[:, 3 * slot_count * owners :].reshape(blocks, width // part, part)

    outgoing = jnp.take(by_block, lists, axis=0, mode="clip")
    arrived = lax.all_to_all(outgoing, "dp", 0, 0, tiled=True)
    grad_rows = arrived.transpose(1, 0, 2, 3).reshape(slot_count, owners, width)

    back = pl.pallas_call(
        rows_kernel,
        out_shape=jax.ShapeDtypeStruct(grad_rows.shape, jnp.bfloat16),
        compiler_params=pltpu.CompilerParams(vmem_limit_bytes=48 * 2**20),
        name="rotate_rows",
    )(grad_rows, basis_all, moved)

    back_out = back.reshape(slot_count, owners, width // part, part).transpose(1, 0, 2, 3)
    returned = lax.all_to_all(back_out, "dp", 0, 0, tiled=True)
    holds = (lists.reshape(-1)[None, :] == jnp.arange(blocks)[:, None]) & live.reshape(-1)[None, :]
    place = jnp.argmax(holds, axis=1)
    placed = jnp.take(
        returned.reshape(owners * slot_count, width // part, part), place, axis=0, mode="clip"
    )
    update = lax.all_to_all(
        placed.reshape(parts, cols_dev // part, part), "tensor", 0, 0, tiled=True
    ).reshape(rows_dev, cols_dev)

    grad_all = lax.all_gather(grad_rows, "tensor", axis=0, tiled=False)
    vmem = pl.BlockSpec(memory_space=pltpu.VMEM)
    new_stats, new_first, new_second = pl.pallas_call(
        state_kernel,
        out_shape=(
            jax.ShapeDtypeStruct(stats.shape[1:], jnp.float32),
            jax.ShapeDtypeStruct(first_moment.shape[1:], jnp.float32),
            jax.ShapeDtypeStruct(second_moment.shape[1:], jnp.float32),
        ),
        in_specs=[pl.BlockSpec(memory_space=pltpu.SMEM)] + [vmem] * 5,
        out_specs=(vmem,) * 3,
        compiler_params=pltpu.CompilerParams(vmem_limit_bytes=48 * 2**20),
        name="new_state",
    )(block_counts, grad_all, basis[0], stats[0], first_moment[0], second_moment[0])
    return (update, new_stats[None], new_first[None], new_second[None])


def solution(mesh):
    placed = (
        P("dp", "tensor"),
        P("dp", None),
        P("dp"),
        P("dp", None, None, "tensor"),
        P("dp", None, None, "tensor"),
        P("dp", None, None, "tensor"),
        P("dp", None, None, "tensor"),
    )
    return jax.shard_map(
        on_device,
        mesh=mesh,
        in_specs=placed,
        out_specs=(
            P("dp", "tensor"),
            P("dp", None, None, "tensor"),
            P("dp", None, None, "tensor"),
            P("dp", None, None, "tensor"),
        ),
        check_vma=False,
    )
```

```python
import jax
import jax.numpy as jnp
from jax import lax
from jax.experimental import pallas as pl
from jax.experimental.pallas import tpu as pltpu
from jax.sharding import PartitionSpec as P

STEP = 10


beta_one = 0.9
beta_two = 0.95
beta_stat = 0.95
epsilon = 1e-08
bias_one = 1.0 - beta_one**STEP
bias_two = 1.0 - beta_two**STEP

GROUPS = 4


def shifted(x, parts, by):
    return lax.ppermute(x, "tensor", [((i + by) % parts, i) for i in range(parts)])


def pack_kernel(share, after_ref, basis_ref, first_ref, second_ref, to_left_ref, to_right_ref):
    slots, width, _ = basis_ref.shape
    rows = first_ref.shape[1]
    owners = rows // (GROUPS * share)
    me = lax.axis_index("tensor") + GROUPS
    piece = 4 * share * owners

    def put(ref, at, target, s):
        base = lax.rem(target, GROUPS) * share
        for i, source in enumerate((first_ref, second_ref)):
            for r in range(share):
                x = source[s, pl.ds(base + r, owners, stride=GROUPS * share), :]
                high = x.astype(jnp.bfloat16)
                low = (x - high.astype(jnp.float32)).astype(jnp.bfloat16)
                here = at + (2 * i * share + r) * owners
                ref[pl.ds(here, owners), :] = high
                ref[pl.ds(here + share * owners, owners), :] = low

    for ref, far, step in ((to_left_ref, 0, -1), (to_right_ref, 1, 1)):
        ref[pl.ds(0, width), :] = basis_ref[far]
        put(ref, width, me + 2 * step, far)
        ref[pl.ds(width + piece, width), :] = basis_ref[1 - far]
        for s in range(slots):
            put(ref, 2 * width + (1 + s) * piece, me + step, s)


def rows_kernel(
    share, arrived_ref, basis_ref, first_ref, second_ref, right_ref, left_ref, far_right_ref,
    far_left_ref, grad_ref, back_ref, rotated_ref, direction_ref, spread_ref,
):
    slots, rows, width = grad_ref.shape
    part = basis_ref.shape[2]
    pieces = width // part
    owners = rows // share
    base = lax.rem(lax.axis_index("tensor"), GROUPS) * share
    piece = 4 * share * owners
    for s in range(slots):
        far_ref = (far_right_ref, far_left_ref)[s]
        near = 2 * width + (1 + s) * piece
        sources = (
            (right_ref, (0, width + piece)[s], near),
            (left_ref, (width + piece, 0)[s], near),
            (far_ref, 0, width),
        )
        basis = jnp.concatenate(
            [basis_ref[s]] + [ref[pl.ds(at, width), :] for ref, at, _ in sources], axis=1
        )
        spread_ref[s] = arrived_ref[:, s].reshape(rows * pieces, part).astype(jnp.float32)
        grad = jnp.concatenate(
            [spread_ref[s, pl.ds(j, rows, stride=pieces), :] for j in range(pieces)], axis=1
        ).astype(jnp.bfloat16)
        grad_ref[s] = grad
        rotated = jnp.dot(grad, basis, preferred_element_type=jnp.float32)
        for i in range(GROUPS):
            rotated_ref[s, i] = rotated[:, i * part : (i + 1) * part]
            for r in range(share):
                local = pl.ds(r, owners, stride=share)
                if i == 0:
                    here = pl.ds(base + r, owners, stride=GROUPS * share)
                    first, second = first_ref[s, here, :], second_ref[s, here, :]
                else:
                    ref, _, at = sources[i - 1]
                    first, second = (
                        ref[pl.ds(at + (2 * m * share + r) * owners, owners), :].astype(jnp.float32)
                        + ref[
                            pl.ds(at + ((2 * m + 1) * share + r) * owners, owners), :
                        ].astype(jnp.float32)
                        for m in range(2)
                    )
                turned = rotated_ref[s, i, local, :]
                moment_one = beta_one * first + (1.0 - beta_one) * turned
                moment_two = beta_two * second + (1.0 - beta_two) * turned * turned
                direction_ref[s, i, local, :] = (
                    moment_one / bias_one / (jnp.sqrt(moment_two / bias_two) + epsilon)
                )
        direction = jnp.concatenate([direction_ref[s, i] for i in range(GROUPS)], axis=1)
        back = lax.dot_general(
            direction.astype(jnp.bfloat16),
            basis,
            (((1,), (1,)), ((), ())),
            preferred_element_type=jnp.float32,
        )
        for j in range(pieces):
            spread_ref[s, pl.ds(j, rows, stride=pieces), :] = back[:, j * part : (j + 1) * part]
        back_ref[:, s] = (
            spread_ref[s].astype(back_ref.dtype).reshape(owners, share, pieces, part)
        )


def state_kernel(
    share, count_ref, grad_ref, right_ref, left_ref, far_ref, basis_ref, stats_ref, first_ref,
    second_ref, new_stats_ref, new_first_ref, new_second_ref, rotated_ref,
):
    slots, rows, _ = grad_ref.shape
    part = basis_ref.shape[2]
    owners = rows // share
    me = lax.axis_index("tensor")
    start = pl.multiple_of(me * part, part)
    for s in range(slots):
        live = s < count_ref[0]
        sources = (grad_ref.at[s], right_ref.at[s], left_ref.at[s], far_ref.at[s])
        grad = jnp.concatenate([ref[...] for ref in sources], axis=0)
        grad_cols = jnp.concatenate([ref[:, pl.ds(start, part)] for ref in sources], axis=0)
        gram = lax.dot_general(
            grad, grad_cols, (((0,), (0,)), ((), ())), preferred_element_type=jnp.float32
        )
        stats = stats_ref[s]
        new_stats_ref[s] = jnp.where(live, beta_stat * stats + (1.0 - beta_stat) * gram, stats)
        rotated_ref[s] = jnp.dot(grad, basis_ref[s], preferred_element_type=jnp.float32)
        for i, offset in enumerate((0, 1, GROUPS - 1, 2)):
            base = lax.rem(me + offset, GROUPS) * share
            for r in range(share):
                rotated = rotated_ref[s, pl.ds(i * rows + r, owners, stride=share), :]
                here = pl.ds(base + r, owners, stride=GROUPS * share)
                first = first_ref[s, here, :]
                second = second_ref[s, here, :]
                new_first_ref[s, here, :] = jnp.where(
                    live, beta_one * first + (1.0 - beta_one) * rotated, first
                )
                new_second_ref[s, here, :] = jnp.where(
                    live, beta_two * second + (1.0 - beta_two) * rotated * rotated, second
                )


def on_device(gradient, block_list, block_counts, stats, basis, first_moment, second_moment):
    rows_dev, cols_dev = gradient.shape
    slot_count = block_list.shape[1]
    owners = lax.axis_size("dp")
    parts = lax.axis_size("tensor")
    width = stats.shape[2]
    part = stats.shape[3]
    blocks = cols_dev * parts // width
    share = rows_dev // GROUPS
    pieces = cols_dev // part
    vmem = pl.BlockSpec(memory_space=pltpu.VMEM)
    params = pltpu.CompilerParams(vmem_limit_bytes=48 * 2**20)

    def own(kernel):
        return lambda *refs: kernel(share, *refs)

    mine = jnp.concatenate([block_list[0], block_counts])
    is_me = jnp.arange(owners)[:, None] == lax.axis_index("dp")
    flat = lax.psum(jnp.where(is_me, mine[None, :], 0).reshape(-1), "dp")
    table = flat.reshape(owners, slot_count + 1)
    lists = table[:, :slot_count]
    live = jnp.arange(slot_count)[None, :] < table[:, slot_count:]

    groups = gradient.reshape(GROUPS, share, pieces, part).transpose(0, 2, 1, 3)
    leaving = jnp.tile(groups, (parts // GROUPS, 1, 1, 1))
    moved = lax.all_to_all(leaving, "tensor", 0, 0, tiled=True)
    by_block = moved.reshape(blocks, width // part, share, part).transpose(0, 2, 1, 3)

    piece = 4 * share * owners
    sent = jax.ShapeDtypeStruct((2 * width + 3 * piece, part), jnp.bfloat16)
    packed = pl.pallas_call(
        own(pack_kernel),
        out_shape=(sent, sent),
        in_specs=[pl.BlockSpec(memory_space=pl.ANY)] + [vmem] * 3,
        out_specs=(vmem,) * 2,
        compiler_params=params,
        name="pack",
    )(leaving, basis[0], first_moment[0], second_moment[0])
    right, left = shifted(packed[0], parts, 1), shifted(packed[1], parts, -1)
    far = (shifted(x[: width + piece], parts, by) for x, by in ((right, 1), (left, -1)))

    outgoing = jnp.take(by_block, lists, axis=0, mode="clip")
    arrived = lax.all_to_all(outgoing, "dp", 0, 0, tiled=True)
    grad_rows, back = pl.pallas_call(
        own(rows_kernel),
        out_shape=(
            jax.ShapeDtypeStruct((slot_count, owners * share, width), jnp.bfloat16),
            jax.ShapeDtypeStruct(arrived.shape, jnp.bfloat16),
        ),
        scratch_shapes=[
            pltpu.VMEM((slot_count, GROUPS, owners * share, part), jnp.float32),
            pltpu.VMEM((slot_count, GROUPS, owners * share, part), jnp.float32),
            pltpu.VMEM((slot_count, owners * share * (width // part), part), jnp.float32),
        ],
        compiler_params=params,
        name="rotate_rows",
    )(arrived, basis[0], first_moment[0], second_moment[0], right, left, *far)

    returned = lax.all_to_all(back, "dp", 0, 0, tiled=True)
    holds = (lists.reshape(-1)[None, :] == jnp.arange(blocks)[:, None]) & live.reshape(-1)[None, :]
    place = jnp.argmax(holds, axis=1)
    placed = jnp.take(
        returned.reshape(owners * slot_count, share, width // part, part), place, axis=0, mode="clip"
    ).transpose(0, 2, 1, 3)
    partial = lax.all_to_all(
        placed.reshape(parts, pieces, share, part), "tensor", 0, 0, tiled=True
    )
    update = (
        partial.reshape(parts // GROUPS, GROUPS, pieces, share, part)
        .astype(jnp.float32)
        .sum(0)
        .astype(jnp.bfloat16)
        .transpose(0, 2, 1, 3)
        .reshape(rows_dev, cols_dev)
    )

    right_rows, left_rows = shifted(grad_rows, parts, 1), shifted(grad_rows, parts, -1)
    others = right_rows, left_rows, shifted(right_rows, parts, 1)
    new_stats, new_first, new_second = pl.pallas_call(
        own(state_kernel),
        out_shape=(
            jax.ShapeDtypeStruct(stats.shape[1:], jnp.float32),
            jax.ShapeDtypeStruct(first_moment.shape[1:], jnp.float32),
            jax.ShapeDtypeStruct(second_moment.shape[1:], jnp.float32),
        ),
        in_specs=[pl.BlockSpec(memory_space=pltpu.SMEM)] + [vmem] * 8,
        out_specs=(vmem,) * 3,
        scratch_shapes=[pltpu.VMEM((slot_count, GROUPS * owners * share, part), jnp.float32)],
        compiler_params=params,
        cost_estimate=pl.CostEstimate(flops=2**30, bytes_accessed=2**24, transcendentals=0),
        name="new_state",
    )(block_counts, grad_rows, *others, basis[0], stats[0], first_moment[0], second_moment[0])
    return (update, new_stats[None], new_first[None], new_second[None])


def solution(mesh):
    placed = (
        P("dp", "tensor"),
        P("dp", None),
        P("dp"),
        P("dp", None, None, "tensor"),
        P("dp", None, None, "tensor"),
        P("dp", None, None, "tensor"),
        P("dp", None, None, "tensor"),
    )
    return jax.shard_map(
        on_device,
        mesh=mesh,
        in_specs=placed,
        out_specs=(
            P("dp", "tensor"),
            P("dp", None, None, "tensor"),
            P("dp", None, None, "tensor"),
            P("dp", None, None, "tensor"),
        ),
        check_vma=False,
    )
```

```python
import jax
import jax.numpy as jnp
from jax import lax
from jax.experimental import pallas as pl
from jax.experimental.pallas import tpu as pltpu
from jax.sharding import PartitionSpec as P

STEP = 10


beta_one = 0.9
beta_two = 0.95
beta_stat = 0.95
epsilon = 1e-08
bias_one = 1.0 - beta_one**STEP
bias_two = 1.0 - beta_two**STEP

GROUPS = 4
ROWS_VMEM = 58 * 2**20
ROWS_FLOPS = 2**34


def shifted(x, parts, by):
    return lax.ppermute(x, "tensor", [((i + by) % parts, i) for i in range(parts)])


def pack_kernel(share, after_ref, basis_ref, first_ref, second_ref, to_left_ref, to_right_ref):
    slots, width, _ = basis_ref.shape
    rows = first_ref.shape[1]
    owners = rows // (GROUPS * share)
    me = lax.axis_index("tensor") + GROUPS
    piece = 4 * share * owners

    def put(ref, at, target, s):
        base = lax.rem(target, GROUPS) * share
        for i, source in enumerate((first_ref, second_ref)):
            for r in range(share):
                x = source[s, pl.ds(base + r, owners, stride=GROUPS * share), :]
                high = x.astype(jnp.bfloat16)
                low = (x - high.astype(jnp.float32)).astype(jnp.bfloat16)
                here = at + (2 * i * share + r) * owners
                ref[pl.ds(here, owners), :] = high
                ref[pl.ds(here + share * owners, owners), :] = low

    for ref, far, step in ((to_left_ref, 0, -1), (to_right_ref, 1, 1)):
        ref[pl.ds(0, width), :] = basis_ref[far]
        put(ref, width, me + 2 * step, far)
        ref[pl.ds(width + piece, width), :] = basis_ref[1 - far]
        for s in range(slots):
            put(ref, 2 * width + (1 + s) * piece, me + step, s)


def spread_rows(tiles, spread_ref):
    rows, pieces, part = tiles.shape
    spread_ref[...] = tiles.reshape(rows * pieces, part).astype(jnp.float32)
    return jnp.concatenate(
        [spread_ref[pl.ds(j, rows, stride=pieces), :] for j in range(pieces)], axis=1
    ).astype(jnp.bfloat16)


def rows_kernel(
    share, arrived_hbm, basis_hbm, first_hbm, second_hbm, right_hbm, left_hbm, far_right_hbm,
    far_left_hbm, place_hbm, back_ref, rotated_ref, direction_ref, spread_ref, arrived_ref, basis_ref,
    first_ref, second_ref, right_ref, left_ref, far_ref, sems,
):
    owners, slots, _, pieces, part = arrived_ref.shape
    rows = owners * share
    width = pieces * part
    base = lax.rem(lax.axis_index("tensor"), GROUPS) * share
    piece = 4 * share * owners
    stay = width + piece

    def needed(s):
        near = stay + width + s * piece
        yield arrived_hbm.at[:, s], arrived_ref.at[:, s]
        yield basis_hbm.at[s], basis_ref.at[s]
        for hbm, ref, at in ((right_hbm, right_ref, (0, stay)[s]), (left_hbm, left_ref, (stay, 0)[s])):
            for first, size in ((at, width), (near, piece)):
                yield hbm.at[pl.ds(first, size)], ref.at[pl.ds(first, size)]
        yield (far_right_hbm, far_left_hbm)[s], far_ref.at[s]
        yield first_hbm.at[s], first_ref.at[s]
        yield second_hbm.at[s], second_ref.at[s]

    copies = [
        [pltpu.make_async_copy(*ends, sems.at[s, i]) for i, ends in enumerate(needed(s))]
        for s in range(slots)
    ]
    for copy in copies[0] + copies[1]:
        copy.start()
    for s in range(slots):
        for copy in copies[s]:
            copy.wait()
        near = 2 * width + (1 + s) * piece
        sources = (
            (right_ref, (0, width + piece)[s], near),
            (left_ref, (width + piece, 0)[s], near),
            (far_ref.at[s], 0, width),
        )
        basis = jnp.concatenate(
            [basis_ref[s]] + [ref[pl.ds(at, width), :] for ref, at, _ in sources], axis=1
        )
        grad = spread_rows(arrived_ref[:, s].reshape(rows, pieces, part), spread_ref)
        rotated = jnp.dot(grad, basis, preferred_element_type=jnp.float32)
        for i in range(GROUPS):
            rotated_ref[s, i] = rotated[:, i * part : (i + 1) * part]
            for r in range(share):
                local = pl.ds(r, owners, stride=share)
                if i == 0:
                    here = pl.ds(base + r, owners, stride=GROUPS * share)
                    first, second = first_ref[s, here, :], second_ref[s, here, :]
                else:
                    ref, _, at = sources[i - 1]
                    first, second = (
                        ref[pl.ds(at + (2 * m * share + r) * owners, owners), :].astype(jnp.float32)
                        + ref[
                            pl.ds(at + ((2 * m + 1) * share + r) * owners, owners), :
                        ].astype(jnp.float32)
                        for m in range(2)
                    )
                turned = rotated_ref[s, i, local, :]
                moment_one = beta_one * first + (1.0 - beta_one) * turned
                moment_two = beta_two * second + (1.0 - beta_two) * turned * turned
                direction_ref[s, i, local, :] = (
                    moment_one / bias_one / (jnp.sqrt(moment_two / bias_two) + epsilon)
                )
        direction = jnp.concatenate([direction_ref[s, i] for i in range(GROUPS)], axis=1)
        back = lax.dot_general(
            direction.astype(jnp.bfloat16),
            basis,
            (((1,), (1,)), ((), ())),
            preferred_element_type=jnp.float32,
        )
        for j in range(pieces):
            spread_ref[pl.ds(j, rows, stride=pieces), :] = back[:, j * part : (j + 1) * part]
        back_ref[:, s] = (
            spread_ref[...].astype(back_ref.dtype).reshape(owners, share, pieces, part)
        )


def near_kernel(
    share, count_ref, grad_ref, right_ref, left_ref, basis_ref, stats_ref, first_ref, second_ref,
    new_stats_ref, new_first_ref, new_second_ref, rotated_ref, spread_ref, all_ref,
):
    owners, slots, _, pieces, part = grad_ref.shape
    rows = owners * share
    me = lax.axis_index("tensor")
    start = pl.multiple_of(me * part, part)
    for s in range(slots):
        live = s < count_ref[0]
        for i, ref in enumerate((grad_ref, right_ref, left_ref)):
            all_ref[s, pl.ds(i * rows, rows), :] = spread_rows(
                ref[:, s].reshape(rows, pieces, part), spread_ref
            )
        grad = all_ref[s]
        grad_cols = all_ref[s, :, pl.ds(start, part)]
        gram = lax.dot_general(
            grad, grad_cols, (((0,), (0,)), ((), ())), preferred_element_type=jnp.float32
        )
        stats = stats_ref[s]
        new_stats_ref[s] = jnp.where(live, beta_stat * stats + (1.0 - beta_stat) * gram, stats)
        rotated_ref[s] = jnp.dot(grad, basis_ref[s], preferred_element_type=jnp.float32)
        for i, offset in enumerate((0, 1, GROUPS - 1)):
            base = lax.rem(me + offset, GROUPS) * share
            for r in range(share):
                rotated = rotated_ref[s, pl.ds(i * rows + r, owners, stride=share), :]
                here = pl.ds(base + r, owners, stride=GROUPS * share)
                first = first_ref[s, here, :]
                second = second_ref[s, here, :]
                new_first_ref[s, here, :] = jnp.where(
                    live, beta_one * first + (1.0 - beta_one) * rotated, first
                )
                new_second_ref[s, here, :] = jnp.where(
                    live, beta_two * second + (1.0 - beta_two) * rotated * rotated, second
                )
        base = lax.rem(me + 2, GROUPS) * share
        for r in range(share):
            here = pl.ds(base + r, owners, stride=GROUPS * share)
            new_first_ref[s, here, :] = first_ref[s, here, :]
            new_second_ref[s, here, :] = second_ref[s, here, :]


def far_kernel(
    share, count_ref, far_ref, basis_ref, stats_ref, first_ref, second_ref,
    new_stats_hbm, new_first_hbm, new_second_hbm,
    new_stats_ref, new_first_ref, new_second_ref, rotated_ref, spread_ref, grad_ref, sems,
):
    owners, slots, _, pieces, part = far_ref.shape
    rows = owners * share
    me = lax.axis_index("tensor")
    start = pl.multiple_of(me * part, part)
    base = lax.rem(me + 2, GROUPS) * share
    copies = []
    for s in range(slots):
        live = s < count_ref[0]
        grad_ref[s] = spread_rows(far_ref[:, s].reshape(rows, pieces, part), spread_ref)
        gram = lax.dot_general(
            grad_ref[s],
            grad_ref[s, :, pl.ds(start, part)],
            (((0,), (0,)), ((), ())),
            preferred_element_type=jnp.float32,
        )
        stats = stats_ref[s]
        new_stats_ref[s] = jnp.where(live, stats + (1.0 - beta_stat) * gram, stats)
        rotated_ref[s] = jnp.dot(grad_ref[s], basis_ref[s], preferred_element_type=jnp.float32)
        new_first_ref[s] = first_ref[s]
        new_second_ref[s] = second_ref[s]
        for r in range(share):
            rotated = rotated_ref[s, pl.ds(r, owners, stride=share), :]
            here = pl.ds(base + r, owners, stride=GROUPS * share)
            first = first_ref[s, here, :]
            second = second_ref[s, here, :]
            new_first_ref[s, here, :] = jnp.where(
                live, beta_one * first + (1.0 - beta_one) * rotated, first
            )
            new_second_ref[s, here, :] = jnp.where(
                live, beta_two * second + (1.0 - beta_two) * rotated * rotated, second
            )
        for i, (ref, hbm) in enumerate((
            (new_stats_ref, new_stats_hbm),
            (new_first_ref, new_first_hbm),
            (new_second_ref, new_second_hbm),
        )):
            copy = pltpu.make_async_copy(ref.at[s], hbm.at[s], sems.at[s, i])
            copy.start()
            copies.append(copy)
    for copy in copies:
        copy.wait()


def add_kernel(partial_ref, update_ref):
    groups, share = GROUPS, partial_ref.shape[2]
    pieces, part = partial_ref.shape[1], partial_ref.shape[3]
    total = partial_ref[:groups].astype(jnp.float32) + partial_ref[groups:].astype(jnp.float32)
    for c in range(pieces):
        update_ref[:, c * part : (c + 1) * part] = (
            total[:, c].reshape(groups * share, part).astype(update_ref.dtype)
        )


def on_device(gradient, block_list, block_counts, stats, basis, first_moment, second_moment):
    rows_dev, cols_dev = gradient.shape
    slot_count = block_list.shape[1]
    owners = lax.axis_size("dp")
    parts = lax.axis_size("tensor")
    width = stats.shape[2]
    part = stats.shape[3]
    blocks = cols_dev * parts // width
    share = rows_dev // GROUPS
    pieces = cols_dev // part
    vmem = pl.BlockSpec(memory_space=pltpu.VMEM)
    params = pltpu.CompilerParams(vmem_limit_bytes=24 * 2**20)

    def own(kernel):
        return lambda *refs: kernel(share, *refs)

    mine = jnp.concatenate([block_list[0], block_counts])
    is_me = jnp.arange(owners)[:, None] == lax.axis_index("dp")
    flat = lax.psum(jnp.where(is_me, mine[None, :], 0).reshape(-1), "dp")
    table = flat.reshape(owners, slot_count + 1)
    lists = table[:, :slot_count]
    live = jnp.arange(slot_count)[None, :] < table[:, slot_count:]

    groups = gradient.reshape(GROUPS, share, pieces, part).transpose(0, 2, 1, 3)
    leaving = jnp.tile(groups, (parts // GROUPS, 1, 1, 1))
    moved = lax.all_to_all(leaving, "tensor", 0, 0, tiled=True)
    by_block = moved.reshape(blocks, width // part, share, part).transpose(0, 2, 1, 3)

    piece = 4 * share * owners
    sent = jax.ShapeDtypeStruct((2 * width + 3 * piece, part), jnp.bfloat16)
    packed = pl.pallas_call(
        own(pack_kernel),
        out_shape=(sent, sent),
        in_specs=[pl.BlockSpec(memory_space=pl.ANY)] + [vmem] * 3,
        out_specs=(vmem,) * 2,
        compiler_params=params,
        name="pack",
    )(leaving, basis[0], first_moment[0], second_moment[0])
    right, left = shifted(packed[0], parts, 1), shifted(packed[1], parts, -1)
    far = (shifted(x[: width + piece], parts, by) for x, by in ((right, 1), (left, -1)))

    outgoing = jnp.take(by_block, lists, axis=0, mode="clip")
    arrived = lax.all_to_all(outgoing, "dp", 0, 0, tiled=True)
    holds = (lists.reshape(-1)[None, :] == jnp.arange(blocks)[:, None]) & live.reshape(-1)[None, :]
    place = jnp.argmax(holds, axis=1)
    rows = owners * share
    operands = (arrived, basis[0], first_moment[0], second_moment[0], right, left, *far)
    back = pl.pallas_call(
        own(rows_kernel),
        out_shape=jax.ShapeDtypeStruct(arrived.shape, jnp.bfloat16),
        in_specs=[pl.BlockSpec(memory_space=pl.ANY)] * (len(operands) + 1),
        out_specs=vmem,
        scratch_shapes=[
            pltpu.VMEM((slot_count, GROUPS, rows, part), jnp.float32),
            pltpu.VMEM((slot_count, GROUPS, rows, part), jnp.float32),
            pltpu.VMEM((rows * (width // part), part), jnp.float32),
            *(pltpu.VMEM(x.shape, x.dtype) for x in operands[:6]),
            pltpu.VMEM((slot_count, width + piece, part), jnp.bfloat16),
            pltpu.SemaphoreType.DMA((slot_count, len(operands) + 1)),
        ],
        compiler_params=pltpu.CompilerParams(vmem_limit_bytes=ROWS_VMEM),
        cost_estimate=pl.CostEstimate(flops=ROWS_FLOPS, bytes_accessed=2**23, transcendentals=0),
        name="rotate_rows",
    )(*operands, place)

    returned = lax.all_to_all(back, "dp", 0, 0, tiled=True)
    placed = jnp.take(
        returned.reshape(owners * slot_count, share, width // part, part), place, axis=0, mode="clip"
    ).transpose(0, 2, 1, 3)
    partial = lax.all_to_all(
        placed.reshape(parts, pieces, share, part), "tensor", 0, 0, tiled=True
    )
    update = pl.pallas_call(
        add_kernel,
        out_shape=jax.ShapeDtypeStruct(gradient.shape, gradient.dtype),
        compiler_params=params,
        name="add",
    )(partial)

    right_rows, left_rows = shifted(arrived, parts, 1), shifted(arrived, parts, -1)
    far_rows = shifted(right_rows, parts, 1)
    states = (stats[0], first_moment[0], second_moment[0])
    shapes = tuple(jax.ShapeDtypeStruct(x.shape, jnp.float32) for x in states)
    smem = pl.BlockSpec(memory_space=pltpu.SMEM)
    spread = pltpu.VMEM((rows * (width // part), part), jnp.float32)
    near = pl.pallas_call(
        own(near_kernel),
        out_shape=shapes,
        in_specs=[smem] + [vmem] * 7,
        out_specs=(vmem,) * 3,
        scratch_shapes=[
            pltpu.VMEM((slot_count, 3 * rows, part), jnp.float32),
            spread,
            pltpu.VMEM((slot_count, 3 * rows, width), jnp.bfloat16),
        ],
        compiler_params=params,
        cost_estimate=pl.CostEstimate(flops=2**32, bytes_accessed=2**24, transcendentals=0),
        name="near_state",
    )(block_counts, arrived, right_rows, left_rows, basis[0], *states)
    new_stats, new_first, new_second = pl.pallas_call(
        own(far_kernel),
        out_shape=shapes,
        in_specs=[smem] + [vmem] * 5,
        out_specs=(pl.BlockSpec(memory_space=pl.ANY),) * 3,
        scratch_shapes=[
            *(pltpu.VMEM(x.shape, x.dtype) for x in shapes),
            pltpu.VMEM((slot_count, rows, part), jnp.float32),
            spread,
            pltpu.VMEM((slot_count, rows, width), jnp.bfloat16),
            pltpu.SemaphoreType.DMA((slot_count, 3)),
        ],
        compiler_params=params,
        name="far_state",
    )(block_counts, far_rows, basis[0], *near)
    return (update, new_stats[None], new_first[None], new_second[None])


def solution(mesh):
    placed = (
        P("dp", "tensor"),
        P("dp", None),
        P("dp"),
        P("dp", None, None, "tensor"),
        P("dp", None, None, "tensor"),
        P("dp", None, None, "tensor"),
        P("dp", None, None, "tensor"),
    )
    return jax.shard_map(
        on_device,
        mesh=mesh,
        in_specs=placed,
        out_specs=(
            P("dp", "tensor"),
            P("dp", None, None, "tensor"),
            P("dp", None, None, "tensor"),
            P("dp", None, None, "tensor"),
        ),
        check_vma=False,
    )
```

```python
import jax
import jax.numpy as jnp
from jax import lax
from jax.experimental import pallas as pl
from jax.experimental.pallas import tpu as pltpu
from jax.sharding import PartitionSpec as P

STEP = 10


beta_one = 0.9
beta_two = 0.95
beta_stat = 0.95
epsilon = 1e-08
bias_one = 1.0 - beta_one**STEP
bias_two = 1.0 - beta_two**STEP

GROUPS = 4
ROWS_VMEM = 58 * 2**20
ROWS_FLOPS = 2**34


def shifted(x, parts, by):
    return lax.ppermute(x, "tensor", [((i + by) % parts, i) for i in range(parts)])


def list_kernel(list_ref, count_ref, after_ref, sent_ref):
    slots = list_ref.shape[1]
    place = lax.broadcasted_iota(jnp.int32, sent_ref.shape, 2)
    entry = jnp.where(place == slots, count_ref[0], 0)
    for s in range(slots):
        entry = jnp.where(place == s, list_ref[0, s], entry)
    sent_ref[...] = entry


def pack_kernel(share, after_ref, basis_ref, first_ref, second_ref, to_left_ref, to_right_ref):
    slots, width, _ = basis_ref.shape
    rows = first_ref.shape[1]
    owners = rows // (GROUPS * share)
    me = lax.axis_index("tensor") + GROUPS
    piece = 4 * share * owners

    def put(ref, at, target, s):
        base = lax.rem(target, GROUPS) * share
        for i, source in enumerate((first_ref, second_ref)):
            for r in range(share):
                x = source[s, pl.ds(base + r, owners, stride=GROUPS * share), :]
                high = x.astype(jnp.bfloat16)
                low = (x - high.astype(jnp.float32)).astype(jnp.bfloat16)
                here = at + (2 * i * share + r) * owners
                ref[pl.ds(here, owners), :] = high
                ref[pl.ds(here + share * owners, owners), :] = low

    for ref, far, step in ((to_left_ref, 0, -1), (to_right_ref, 1, 1)):
        ref[pl.ds(0, width), :] = basis_ref[far]
        put(ref, width, me + 2 * step, far)
        ref[pl.ds(width + piece, width), :] = basis_ref[1 - far]
        for s in range(slots):
            put(ref, 2 * width + (1 + s) * piece, me + step, s)


def spread_rows(tiles, spread_ref):
    rows, pieces, part = tiles.shape
    spread_ref[...] = tiles.reshape(rows * pieces, part).astype(jnp.float32)
    return jnp.concatenate(
        [spread_ref[pl.ds(j, rows, stride=pieces), :] for j in range(pieces)], axis=1
    ).astype(jnp.bfloat16)


def rows_kernel(
    share, arrived_hbm, basis_hbm, first_hbm, second_hbm, right_hbm, left_hbm, far_right_hbm,
    far_left_hbm, place_hbm, back_ref, rotated_ref, direction_ref, spread_ref, arrived_ref, basis_ref,
    first_ref, second_ref, right_ref, left_ref, far_ref, sems,
):
    owners, slots, _, pieces, part = arrived_ref.shape
    rows = owners * share
    width = pieces * part
    base = lax.rem(lax.axis_index("tensor"), GROUPS) * share
    piece = 4 * share * owners
    stay = width + piece

    def needed(s):
        near = stay + width + s * piece
        yield arrived_hbm.at[:, s], arrived_ref.at[:, s]
        yield basis_hbm.at[s], basis_ref.at[s]
        for hbm, ref, at in ((right_hbm, right_ref, (0, stay)[s]), (left_hbm, left_ref, (stay, 0)[s])):
            for first, size in ((at, width), (near, piece)):
                yield hbm.at[pl.ds(first, size)], ref.at[pl.ds(first, size)]
        yield (far_right_hbm, far_left_hbm)[s], far_ref.at[s]
        yield first_hbm.at[s], first_ref.at[s]
        yield second_hbm.at[s], second_ref.at[s]

    copies = [
        [pltpu.make_async_copy(*ends, sems.at[s, i]) for i, ends in enumerate(needed(s))]
        for s in range(slots)
    ]
    for copy in copies[0] + copies[1]:
        copy.start()
    for s in range(slots):
        for copy in copies[s]:
            copy.wait()
        near = 2 * width + (1 + s) * piece
        sources = (
            (right_ref, (0, width + piece)[s], near),
            (left_ref, (width + piece, 0)[s], near),
            (far_ref.at[s], 0, width),
        )
        basis = jnp.concatenate(
            [basis_ref[s]] + [ref[pl.ds(at, width), :] for ref, at, _ in sources], axis=1
        )
        grad = spread_rows(arrived_ref[:, s].reshape(rows, pieces, part), spread_ref)
        rotated = jnp.dot(grad, basis, preferred_element_type=jnp.float32)
        for i in range(GROUPS):
            rotated_ref[s, i] = rotated[:, i * part : (i + 1) * part]
            for r in range(share):
                local = pl.ds(r, owners, stride=share)
                if i == 0:
                    here = pl.ds(base + r, owners, stride=GROUPS * share)
                    first, second = first_ref[s, here, :], second_ref[s, here, :]
                else:
                    ref, _, at = sources[i - 1]
                    first, second = (
                        ref[pl.ds(at + (2 * m * share + r) * owners, owners), :].astype(jnp.float32)
                        + ref[
                            pl.ds(at + ((2 * m + 1) * share + r) * owners, owners), :
                        ].astype(jnp.float32)
                        for m in range(2)
                    )
                turned = rotated_ref[s, i, local, :]
                moment_one = beta_one * first + (1.0 - beta_one) * turned
                moment_two = beta_two * second + (1.0 - beta_two) * turned * turned
                direction_ref[s, i, local, :] = (
                    moment_one / bias_one / (jnp.sqrt(moment_two / bias_two) + epsilon)
                )
        direction = jnp.concatenate([direction_ref[s, i] for i in range(GROUPS)], axis=1)
        back = lax.dot_general(
            direction.astype(jnp.bfloat16),
            basis,
            (((1,), (1,)), ((), ())),
            preferred_element_type=jnp.float32,
        )
        for j in range(pieces):
            spread_ref[pl.ds(j, rows, stride=pieces), :] = back[:, j * part : (j + 1) * part]
        back_ref[:, s] = (
            spread_ref[...].astype(back_ref.dtype).reshape(owners, share, pieces, part)
        )


def near_kernel(
    share, count_ref, grad_ref, right_ref, left_ref, basis_ref, stats_ref, first_ref, second_ref,
    new_stats_ref, new_first_ref, new_second_ref, rotated_ref, spread_ref, all_ref,
):
    owners, slots, _, pieces, part = grad_ref.shape
    rows = owners * share
    me = lax.axis_index("tensor")
    start = pl.multiple_of(me * part, part)
    for s in range(slots):
        live = s < count_ref[0]
        for i, ref in enumerate((grad_ref, right_ref, left_ref)):
            all_ref[s, pl.ds(i * rows, rows), :] = spread_rows(
                ref[:, s].reshape(rows, pieces, part), spread_ref
            )
        grad = all_ref[s]
        grad_cols = all_ref[s, :, pl.ds(start, part)]
        gram = lax.dot_general(
            grad, grad_cols, (((0,), (0,)), ((), ())), preferred_element_type=jnp.float32
        )
        stats = stats_ref[s]
        new_stats_ref[s] = jnp.where(live, beta_stat * stats + (1.0 - beta_stat) * gram, stats)
        rotated_ref[s] = jnp.dot(grad, basis_ref[s], preferred_element_type=jnp.float32)
        for i, offset in enumerate((0, 1, GROUPS - 1)):
            base = lax.rem(me + offset, GROUPS) * share
            for r in range(share):
                rotated = rotated_ref[s, pl.ds(i * rows + r, owners, stride=share), :]
                here = pl.ds(base + r, owners, stride=GROUPS * share)
                first = first_ref[s, here, :]
                second = second_ref[s, here, :]
                new_first_ref[s, here, :] = jnp.where(
                    live, beta_one * first + (1.0 - beta_one) * rotated, first
                )
                new_second_ref[s, here, :] = jnp.where(
                    live, beta_two * second + (1.0 - beta_two) * rotated * rotated, second
                )
        base = lax.rem(me + 2, GROUPS) * share
        for r in range(share):
            here = pl.ds(base + r, owners, stride=GROUPS * share)
            new_first_ref[s, here, :] = first_ref[s, here, :]
            new_second_ref[s, here, :] = second_ref[s, here, :]


def far_kernel(
    share, count_ref, far_ref, basis_ref, stats_ref, first_ref, second_ref,
    new_stats_hbm, new_first_hbm, new_second_hbm,
    new_stats_ref, new_first_ref, new_second_ref, rotated_ref, spread_ref, grad_ref, sems,
):
    owners, slots, _, pieces, part = far_ref.shape
    rows = owners * share
    me = lax.axis_index("tensor")
    start = pl.multiple_of(me * part, part)
    base = lax.rem(me + 2, GROUPS) * share
    copies = []
    for s in range(slots):
        live = s < count_ref[0]
        grad_ref[s] = spread_rows(far_ref[:, s].reshape(rows, pieces, part), spread_ref)
        gram = lax.dot_general(
            grad_ref[s],
            grad_ref[s, :, pl.ds(start, part)],
            (((0,), (0,)), ((), ())),
            preferred_element_type=jnp.float32,
        )
        stats = stats_ref[s]
        new_stats_ref[s] = jnp.where(live, stats + (1.0 - beta_stat) * gram, stats)
        rotated_ref[s] = jnp.dot(grad_ref[s], basis_ref[s], preferred_element_type=jnp.float32)
        new_first_ref[s] = first_ref[s]
        new_second_ref[s] = second_ref[s]
        for r in range(share):
            rotated = rotated_ref[s, pl.ds(r, owners, stride=share), :]
            here = pl.ds(base + r, owners, stride=GROUPS * share)
            first = first_ref[s, here, :]
            second = second_ref[s, here, :]
            new_first_ref[s, here, :] = jnp.where(
                live, beta_one * first + (1.0 - beta_one) * rotated, first
            )
            new_second_ref[s, here, :] = jnp.where(
                live, beta_two * second + (1.0 - beta_two) * rotated * rotated, second
            )
        for i, (ref, hbm) in enumerate((
            (new_stats_ref, new_stats_hbm),
            (new_first_ref, new_first_hbm),
            (new_second_ref, new_second_hbm),
        )):
            copy = pltpu.make_async_copy(ref.at[s], hbm.at[s], sems.at[s, i])
            copy.start()
            copies.append(copy)
    for copy in copies:
        copy.wait()


def add_kernel(partial_ref, update_ref):
    groups, share = GROUPS, partial_ref.shape[2]
    pieces, part = partial_ref.shape[1], partial_ref.shape[3]
    total = partial_ref[:groups].astype(jnp.float32) + partial_ref[groups:].astype(jnp.float32)
    for c in range(pieces):
        update_ref[:, c * part : (c + 1) * part] = (
            total[:, c].reshape(groups * share, part).astype(update_ref.dtype)
        )


def on_device(gradient, block_list, block_counts, stats, basis, first_moment, second_moment):
    rows_dev, cols_dev = gradient.shape
    slot_count = block_list.shape[1]
    owners = lax.axis_size("dp")
    parts = lax.axis_size("tensor")
    width = stats.shape[2]
    part = stats.shape[3]
    blocks = cols_dev * parts // width
    share = rows_dev // GROUPS
    pieces = cols_dev // part
    vmem = pl.BlockSpec(memory_space=pltpu.VMEM)
    smem = pl.BlockSpec(memory_space=pltpu.SMEM)
    params = pltpu.CompilerParams(vmem_limit_bytes=24 * 2**20)

    def own(kernel):
        return lambda *refs: kernel(share, *refs)

    groups = gradient.reshape(GROUPS, share, pieces, part).transpose(0, 2, 1, 3)
    leaving = jnp.tile(groups, (parts // GROUPS, 1, 1, 1))
    moved = lax.all_to_all(leaving, "tensor", 0, 0, tiled=True)
    by_block = moved.reshape(blocks, width // part, share, part).transpose(0, 2, 1, 3)

    mine = pl.pallas_call(
        list_kernel,
        out_shape=jax.ShapeDtypeStruct((owners, 1, part), jnp.int32),
        in_specs=[smem, smem, pl.BlockSpec(memory_space=pl.ANY)],
        out_specs=vmem,
        compiler_params=params,
        name="list",
    )(block_list, block_counts, moved)
    table = lax.all_to_all(mine, "dp", 0, 0, tiled=True).reshape(owners, part)
    lists = table[:, :slot_count]
    live = jnp.arange(slot_count)[None, :] < table[:, slot_count : slot_count + 1]

    piece = 4 * share * owners
    sent = jax.ShapeDtypeStruct((2 * width + 3 * piece, part), jnp.bfloat16)
    packed = pl.pallas_call(
        own(pack_kernel),
        out_shape=(sent, sent),
        in_specs=[pl.BlockSpec(memory_space=pl.ANY)] + [vmem] * 3,
        out_specs=(vmem,) * 2,
        compiler_params=params,
        name="pack",
    )(leaving, basis[0], first_moment[0], second_moment[0])
    right, left = shifted(packed[0], parts, 1), shifted(packed[1], parts, -1)
    far = (shifted(x[: width + piece], parts, by) for x, by in ((right, 1), (left, -1)))

    outgoing = jnp.take(by_block, lists, axis=0, mode="clip")
    arrived = lax.all_to_all(outgoing, "dp", 0, 0, tiled=True)
    holds = (lists.reshape(-1)[None, :] == jnp.arange(blocks)[:, None]) & live.reshape(-1)[None, :]
    place = jnp.argmax(holds, axis=1)
    rows = owners * share
    operands = (arrived, basis[0], first_moment[0], second_moment[0], right, left, *far)
    back = pl.pallas_call(
        own(rows_kernel),
        out_shape=jax.ShapeDtypeStruct(arrived.shape, jnp.bfloat16),
        in_specs=[pl.BlockSpec(memory_space=pl.ANY)] * (len(operands) + 1),
        out_specs=vmem,
        scratch_shapes=[
            pltpu.VMEM((slot_count, GROUPS, rows, part), jnp.float32),
            pltpu.VMEM((slot_count, GROUPS, rows, part), jnp.float32),
            pltpu.VMEM((rows * (width // part), part), jnp.float32),
            *(pltpu.VMEM(x.shape, x.dtype) for x in operands[:6]),
            pltpu.VMEM((slot_count, width + piece, part), jnp.bfloat16),
            pltpu.SemaphoreType.DMA((slot_count, len(operands) + 1)),
        ],
        compiler_params=pltpu.CompilerParams(vmem_limit_bytes=ROWS_VMEM),
        cost_estimate=pl.CostEstimate(flops=ROWS_FLOPS, bytes_accessed=2**23, transcendentals=0),
        name="rotate_rows",
    )(*operands, place)

    returned = lax.all_to_all(back, "dp", 0, 0, tiled=True)
    placed = jnp.take(
        returned.reshape(owners * slot_count, share, width // part, part), place, axis=0, mode="clip"
    ).transpose(0, 2, 1, 3)
    partial = lax.all_to_all(
        placed.reshape(parts, pieces, share, part), "tensor", 0, 0, tiled=True
    )
    update = pl.pallas_call(
        add_kernel,
        out_shape=jax.ShapeDtypeStruct(gradient.shape, gradient.dtype),
        compiler_params=params,
        name="add",
    )(partial)

    right_rows, left_rows = shifted(arrived, parts, 1), shifted(arrived, parts, -1)
    far_rows = shifted(right_rows, parts, 1)
    states = (stats[0], first_moment[0], second_moment[0])
    shapes = tuple(jax.ShapeDtypeStruct(x.shape, jnp.float32) for x in states)
    spread = pltpu.VMEM((rows * (width // part), part), jnp.float32)
    near = pl.pallas_call(
        own(near_kernel),
        out_shape=shapes,
        in_specs=[smem] + [vmem] * 7,
        out_specs=(vmem,) * 3,
        scratch_shapes=[
            pltpu.VMEM((slot_count, 3 * rows, part), jnp.float32),
            spread,
            pltpu.VMEM((slot_count, 3 * rows, width), jnp.bfloat16),
        ],
        compiler_params=params,
        cost_estimate=pl.CostEstimate(flops=2**32, bytes_accessed=2**24, transcendentals=0),
        name="near_state",
    )(block_counts, arrived, right_rows, left_rows, basis[0], *states)
    new_stats, new_first, new_second = pl.pallas_call(
        own(far_kernel),
        out_shape=shapes,
        in_specs=[smem] + [vmem] * 5,
        out_specs=(pl.BlockSpec(memory_space=pl.ANY),) * 3,
        scratch_shapes=[
            *(pltpu.VMEM(x.shape, x.dtype) for x in shapes),
            pltpu.VMEM((slot_count, rows, part), jnp.float32),
            spread,
            pltpu.VMEM((slot_count, rows, width), jnp.bfloat16),
            pltpu.SemaphoreType.DMA((slot_count, 3)),
        ],
        compiler_params=params,
        name="far_state",
    )(block_counts, far_rows, basis[0], *near)
    return (update, new_stats[None], new_first[None], new_second[None])


def solution(mesh):
    placed = (
        P("dp", "tensor"),
        P("dp", None),
        P("dp"),
        P("dp", None, None, "tensor"),
        P("dp", None, None, "tensor"),
        P("dp", None, None, "tensor"),
        P("dp", None, None, "tensor"),
    )
    return jax.shard_map(
        on_device,
        mesh=mesh,
        in_specs=placed,
        out_specs=(
            P("dp", "tensor"),
            P("dp", None, None, "tensor"),
            P("dp", None, None, "tensor"),
            P("dp", None, None, "tensor"),
        ),
        check_vma=False,
    )
```

```python
import jax
import jax.numpy as jnp
from jax import lax
from jax.experimental import pallas as pl
from jax.experimental.pallas import tpu as pltpu
from jax.sharding import PartitionSpec as P

STEP = 10


beta_one = 0.9
beta_two = 0.95
beta_stat = 0.95
epsilon = 1e-08
bias_one = 1.0 - beta_one**STEP
bias_two = 1.0 - beta_two**STEP

GROUPS = 4
ROWS_VMEM = 58 * 2**20
ROWS_FLOPS = 2**34


def shifted(x, parts, by):
    return lax.ppermute(x, "tensor", [((i + by) % parts, i) for i in range(parts)])


def after_kernel(sent_ref, after_ref, out_ref):
    pass


def list_kernel(list_ref, count_ref, sent_ref):
    slots = list_ref.shape[1]
    place = lax.broadcasted_iota(jnp.int32, sent_ref.shape, 2)
    entry = jnp.where(place == slots, count_ref[0], 0)
    for s in range(slots):
        entry = jnp.where(place == s, list_ref[0, s], entry)
    sent_ref[...] = entry


def pack_kernel(share, after_ref, basis_ref, first_ref, second_ref, to_left_ref, to_right_ref):
    slots, width, _ = basis_ref.shape
    rows = first_ref.shape[1]
    owners = rows // (GROUPS * share)
    me = lax.axis_index("tensor") + GROUPS
    piece = 4 * share * owners

    def put(ref, at, target, s):
        base = lax.rem(target, GROUPS) * share
        for i, source in enumerate((first_ref, second_ref)):
            for r in range(share):
                x = source[s, pl.ds(base + r, owners, stride=GROUPS * share), :]
                high = x.astype(jnp.bfloat16)
                low = (x - high.astype(jnp.float32)).astype(jnp.bfloat16)
                here = at + (2 * i * share + r) * owners
                ref[pl.ds(here, owners), :] = high
                ref[pl.ds(here + share * owners, owners), :] = low

    for ref, far, step in ((to_left_ref, 0, -1), (to_right_ref, 1, 1)):
        ref[pl.ds(0, width), :] = basis_ref[far]
        put(ref, width, me + 2 * step, far)
        ref[pl.ds(width + piece, width), :] = basis_ref[1 - far]
        for s in range(slots):
            put(ref, 2 * width + (1 + s) * piece, me + step, s)


def spread_rows(tiles, spread_ref):
    rows, pieces, part = tiles.shape
    spread_ref[...] = tiles.reshape(rows * pieces, part).astype(jnp.float32)
    return jnp.concatenate(
        [spread_ref[pl.ds(j, rows, stride=pieces), :] for j in range(pieces)], axis=1
    ).astype(jnp.bfloat16)


def rows_kernel(
    share, arrived_hbm, basis_hbm, first_hbm, second_hbm, right_hbm, left_hbm, far_right_hbm,
    far_left_hbm, place_hbm, back_ref, rotated_ref, direction_ref, spread_ref, arrived_ref, basis_ref,
    first_ref, second_ref, right_ref, left_ref, far_ref, sems,
):
    owners, slots, _, pieces, part = arrived_ref.shape
    rows = owners * share
    width = pieces * part
    base = lax.rem(lax.axis_index("tensor"), GROUPS) * share
    piece = 4 * share * owners
    stay = width + piece

    def needed(s):
        near = stay + width + s * piece
        yield arrived_hbm.at[:, s], arrived_ref.at[:, s]
        yield basis_hbm.at[s], basis_ref.at[s]
        for hbm, ref, at in ((right_hbm, right_ref, (0, stay)[s]), (left_hbm, left_ref, (stay, 0)[s])):
            for first, size in ((at, width), (near, piece)):
                yield hbm.at[pl.ds(first, size)], ref.at[pl.ds(first, size)]
        yield (far_right_hbm, far_left_hbm)[s], far_ref.at[s]
        yield first_hbm.at[s], first_ref.at[s]
        yield second_hbm.at[s], second_ref.at[s]

    copies = [
        [pltpu.make_async_copy(*ends, sems.at[s, i]) for i, ends in enumerate(needed(s))]
        for s in range(slots)
    ]
    for copy in copies[0] + copies[1]:
        copy.start()
    for s in range(slots):
        for copy in copies[s]:
            copy.wait()
        near = 2 * width + (1 + s) * piece
        sources = (
            (right_ref, (0, width + piece)[s], near),
            (left_ref, (width + piece, 0)[s], near),
            (far_ref.at[s], 0, width),
        )
        basis = jnp.concatenate(
            [basis_ref[s]] + [ref[pl.ds(at, width), :] for ref, at, _ in sources], axis=1
        )
        grad = spread_rows(arrived_ref[:, s].reshape(rows, pieces, part), spread_ref)
        rotated = jnp.dot(grad, basis, preferred_element_type=jnp.float32)
        for i in range(GROUPS):
            rotated_ref[s, i] = rotated[:, i * part : (i + 1) * part]
            for r in range(share):
                local = pl.ds(r, owners, stride=share)
                if i == 0:
                    here = pl.ds(base + r, owners, stride=GROUPS * share)
                    first, second = first_ref[s, here, :], second_ref[s, here, :]
                else:
                    ref, _, at = sources[i - 1]
                    first, second = (
                        ref[pl.ds(at + (2 * m * share + r) * owners, owners), :].astype(jnp.float32)
                        + ref[
                            pl.ds(at + ((2 * m + 1) * share + r) * owners, owners), :
                        ].astype(jnp.float32)
                        for m in range(2)
                    )
                turned = rotated_ref[s, i, local, :]
                moment_one = beta_one * first + (1.0 - beta_one) * turned
                moment_two = beta_two * second + (1.0 - beta_two) * turned * turned
                direction_ref[s, i, local, :] = (
                    moment_one / bias_one / (jnp.sqrt(moment_two / bias_two) + epsilon)
                )
        direction = jnp.concatenate([direction_ref[s, i] for i in range(GROUPS)], axis=1)
        back = lax.dot_general(
            direction.astype(jnp.bfloat16),
            basis,
            (((1,), (1,)), ((), ())),
            preferred_element_type=jnp.float32,
        )
        for j in range(pieces):
            spread_ref[pl.ds(j, rows, stride=pieces), :] = back[:, j * part : (j + 1) * part]
        back_ref[:, s] = (
            spread_ref[...].astype(back_ref.dtype).reshape(owners, share, pieces, part)
        )


def near_kernel(
    share, count_ref, grad_ref, right_ref, left_ref, basis_ref, stats_ref, first_ref, second_ref,
    new_stats_ref, new_first_ref, new_second_ref, rotated_ref, spread_ref, all_ref,
):
    owners, slots, _, pieces, part = grad_ref.shape
    rows = owners * share
    me = lax.axis_index("tensor")
    start = pl.multiple_of(me * part, part)
    for s in range(slots):
        live = s < count_ref[0]
        for i, ref in enumerate((grad_ref, right_ref, left_ref)):
            all_ref[s, pl.ds(i * rows, rows), :] = spread_rows(
                ref[:, s].reshape(rows, pieces, part), spread_ref
            )
        grad = all_ref[s]
        grad_cols = all_ref[s, :, pl.ds(start, part)]
        gram = lax.dot_general(
            grad, grad_cols, (((0,), (0,)), ((), ())), preferred_element_type=jnp.float32
        )
        stats = stats_ref[s]
        new_stats_ref[s] = jnp.where(live, beta_stat * stats + (1.0 - beta_stat) * gram, stats)
        rotated_ref[s] = jnp.dot(grad, basis_ref[s], preferred_element_type=jnp.float32)
        for i, offset in enumerate((0, 1, GROUPS - 1)):
            base = lax.rem(me + offset, GROUPS) * share
            for r in range(share):
                rotated = rotated_ref[s, pl.ds(i * rows + r, owners, stride=share), :]
                here = pl.ds(base + r, owners, stride=GROUPS * share)
                first = first_ref[s, here, :]
                second = second_ref[s, here, :]
                new_first_ref[s, here, :] = jnp.where(
                    live, beta_one * first + (1.0 - beta_one) * rotated, first
                )
                new_second_ref[s, here, :] = jnp.where(
                    live, beta_two * second + (1.0 - beta_two) * rotated * rotated, second
                )
        base = lax.rem(me + 2, GROUPS) * share
        for r in range(share):
            here = pl.ds(base + r, owners, stride=GROUPS * share)
            new_first_ref[s, here, :] = first_ref[s, here, :]
            new_second_ref[s, here, :] = second_ref[s, here, :]


def far_kernel(
    share, count_ref, far_ref, basis_ref, stats_ref, first_ref, second_ref,
    new_stats_hbm, new_first_hbm, new_second_hbm,
    new_stats_ref, new_first_ref, new_second_ref, rotated_ref, spread_ref, grad_ref, sems,
):
    owners, slots, _, pieces, part = far_ref.shape
    rows = owners * share
    me = lax.axis_index("tensor")
    start = pl.multiple_of(me * part, part)
    base = lax.rem(me + 2, GROUPS) * share
    copies = []
    for s in range(slots):
        live = s < count_ref[0]
        grad_ref[s] = spread_rows(far_ref[:, s].reshape(rows, pieces, part), spread_ref)
        gram = lax.dot_general(
            grad_ref[s],
            grad_ref[s, :, pl.ds(start, part)],
            (((0,), (0,)), ((), ())),
            preferred_element_type=jnp.float32,
        )
        stats = stats_ref[s]
        new_stats_ref[s] = jnp.where(live, stats + (1.0 - beta_stat) * gram, stats)
        rotated_ref[s] = jnp.dot(grad_ref[s], basis_ref[s], preferred_element_type=jnp.float32)
        new_first_ref[s] = first_ref[s]
        new_second_ref[s] = second_ref[s]
        for r in range(share):
            rotated = rotated_ref[s, pl.ds(r, owners, stride=share), :]
            here = pl.ds(base + r, owners, stride=GROUPS * share)
            first = first_ref[s, here, :]
            second = second_ref[s, here, :]
            new_first_ref[s, here, :] = jnp.where(
                live, beta_one * first + (1.0 - beta_one) * rotated, first
            )
            new_second_ref[s, here, :] = jnp.where(
                live, beta_two * second + (1.0 - beta_two) * rotated * rotated, second
            )
        for i, (ref, hbm) in enumerate((
            (new_stats_ref, new_stats_hbm),
            (new_first_ref, new_first_hbm),
            (new_second_ref, new_second_hbm),
        )):
            copy = pltpu.make_async_copy(ref.at[s], hbm.at[s], sems.at[s, i])
            copy.start()
            copies.append(copy)
    for copy in copies:
        copy.wait()


def add_kernel(partial_ref, update_ref):
    groups, share = GROUPS, partial_ref.shape[2]
    pieces, part = partial_ref.shape[1], partial_ref.shape[3]
    total = partial_ref[:groups].astype(jnp.float32) + partial_ref[groups:].astype(jnp.float32)
    for c in range(pieces):
        update_ref[:, c * part : (c + 1) * part] = (
            total[:, c].reshape(groups * share, part).astype(update_ref.dtype)
        )


def on_device(gradient, block_list, block_counts, stats, basis, first_moment, second_moment):
    rows_dev, cols_dev = gradient.shape
    slot_count = block_list.shape[1]
    owners = lax.axis_size("dp")
    parts = lax.axis_size("tensor")
    width = stats.shape[2]
    part = stats.shape[3]
    blocks = cols_dev * parts // width
    share = rows_dev // GROUPS
    pieces = cols_dev // part
    vmem = pl.BlockSpec(memory_space=pltpu.VMEM)
    smem = pl.BlockSpec(memory_space=pltpu.SMEM)
    params = pltpu.CompilerParams(vmem_limit_bytes=24 * 2**20)

    def own(kernel):
        return lambda *refs: kernel(share, *refs)

    groups = gradient.reshape(GROUPS, share, pieces, part).transpose(0, 2, 1, 3)
    leaving = jnp.tile(groups, (parts // GROUPS, 1, 1, 1))
    moved = lax.all_to_all(leaving, "tensor", 0, 0, tiled=True)
    by_block = moved.reshape(blocks, width // part, share, part).transpose(0, 2, 1, 3)

    mine = pl.pallas_call(
        list_kernel,
        out_shape=jax.ShapeDtypeStruct((owners, 1, part), jnp.int32),
        in_specs=[smem, smem],
        out_specs=vmem,
        compiler_params=params,
        name="list",
    )(block_list, block_counts)
    mine = pl.pallas_call(
        after_kernel,
        out_shape=jax.ShapeDtypeStruct(mine.shape, mine.dtype),
        in_specs=[pl.BlockSpec(memory_space=pl.ANY)] * 2,
        out_specs=pl.BlockSpec(memory_space=pl.ANY),
        input_output_aliases={0: 0},
        name="after",
    )(mine, moved)
    table = lax.all_to_all(mine, "dp", 0, 0, tiled=True).reshape(owners, part)
    lists = table[:, :slot_count]
    live = jnp.arange(slot_count)[None, :] < table[:, slot_count : slot_count + 1]

    piece = 4 * share * owners
    sent = jax.ShapeDtypeStruct((2 * width + 3 * piece, part), jnp.bfloat16)
    packed = pl.pallas_call(
        own(pack_kernel),
        out_shape=(sent, sent),
        in_specs=[pl.BlockSpec(memory_space=pl.ANY)] + [vmem] * 3,
        out_specs=(vmem,) * 2,
        compiler_params=params,
        name="pack",
    )(leaving, basis[0], first_moment[0], second_moment[0])
    right, left = shifted(packed[0], parts, 1), shifted(packed[1], parts, -1)
    far = (shifted(x[: width + piece], parts, by) for x, by in ((right, 1), (left, -1)))

    outgoing = jnp.take(by_block, lists, axis=0, mode="clip")
    arrived = lax.all_to_all(outgoing, "dp", 0, 0, tiled=True)
    holds = (lists.reshape(-1)[None, :] == jnp.arange(blocks)[:, None]) & live.reshape(-1)[None, :]
    place = jnp.argmax(holds, axis=1)
    rows = owners * share
    operands = (arrived, basis[0], first_moment[0], second_moment[0], right, left, *far)
    back = pl.pallas_call(
        own(rows_kernel),
        out_shape=jax.ShapeDtypeStruct(arrived.shape, jnp.bfloat16),
        in_specs=[pl.BlockSpec(memory_space=pl.ANY)] * (len(operands) + 1),
        out_specs=vmem,
        scratch_shapes=[
            pltpu.VMEM((slot_count, GROUPS, rows, part), jnp.float32),
            pltpu.VMEM((slot_count, GROUPS, rows, part), jnp.float32),
            pltpu.VMEM((rows * (width // part), part), jnp.float32),
            *(pltpu.VMEM(x.shape, x.dtype) for x in operands[:6]),
            pltpu.VMEM((slot_count, width + piece, part), jnp.bfloat16),
            pltpu.SemaphoreType.DMA((slot_count, len(operands) + 1)),
        ],
        compiler_params=pltpu.CompilerParams(vmem_limit_bytes=ROWS_VMEM),
        cost_estimate=pl.CostEstimate(flops=ROWS_FLOPS, bytes_accessed=2**23, transcendentals=0),
        name="rotate_rows",
    )(*operands, place)

    returned = lax.all_to_all(back, "dp", 0, 0, tiled=True)
    placed = jnp.take(
        returned.reshape(owners * slot_count, share, width // part, part), place, axis=0, mode="clip"
    ).transpose(0, 2, 1, 3)
    partial = lax.all_to_all(
        placed.reshape(parts, pieces, share, part), "tensor", 0, 0, tiled=True
    )
    update = pl.pallas_call(
        add_kernel,
        out_shape=jax.ShapeDtypeStruct(gradient.shape, gradient.dtype),
        compiler_params=params,
        name="add",
    )(partial)

    right_rows, left_rows = shifted(arrived, parts, 1), shifted(arrived, parts, -1)
    far_rows = shifted(right_rows, parts, 1)
    states = (stats[0], first_moment[0], second_moment[0])
    shapes = tuple(jax.ShapeDtypeStruct(x.shape, jnp.float32) for x in states)
    spread = pltpu.VMEM((rows * (width // part), part), jnp.float32)
    near = pl.pallas_call(
        own(near_kernel),
        out_shape=shapes,
        in_specs=[smem] + [vmem] * 7,
        out_specs=(vmem,) * 3,
        scratch_shapes=[
            pltpu.VMEM((slot_count, 3 * rows, part), jnp.float32),
            spread,
            pltpu.VMEM((slot_count, 3 * rows, width), jnp.bfloat16),
        ],
        compiler_params=params,
        cost_estimate=pl.CostEstimate(flops=2**32, bytes_accessed=2**24, transcendentals=0),
        name="near_state",
    )(block_counts, arrived, right_rows, left_rows, basis[0], *states)
    new_stats, new_first, new_second = pl.pallas_call(
        own(far_kernel),
        out_shape=shapes,
        in_specs=[smem] + [vmem] * 5,
        out_specs=(pl.BlockSpec(memory_space=pl.ANY),) * 3,
        scratch_shapes=[
            *(pltpu.VMEM(x.shape, x.dtype) for x in shapes),
            pltpu.VMEM((slot_count, rows, part), jnp.float32),
            spread,
            pltpu.VMEM((slot_count, rows, width), jnp.bfloat16),
            pltpu.SemaphoreType.DMA((slot_count, 3)),
        ],
        compiler_params=params,
        name="far_state",
    )(block_counts, far_rows, basis[0], *near)
    return (update, new_stats[None], new_first[None], new_second[None])


def solution(mesh):
    placed = (
        P("dp", "tensor"),
        P("dp", None),
        P("dp"),
        P("dp", None, None, "tensor"),
        P("dp", None, None, "tensor"),
        P("dp", None, None, "tensor"),
        P("dp", None, None, "tensor"),
    )
    return jax.shard_map(
        on_device,
        mesh=mesh,
        in_specs=placed,
        out_specs=(
            P("dp", "tensor"),
            P("dp", None, None, "tensor"),
            P("dp", None, None, "tensor"),
            P("dp", None, None, "tensor"),
        ),
        check_vma=False,
    )
```

```python
import jax
import jax.numpy as jnp
from jax import lax
from jax.experimental import pallas as pl
from jax.experimental.pallas import tpu as pltpu
from jax.sharding import PartitionSpec as P

STEP = 10


beta_one = 0.9
beta_two = 0.95
beta_stat = 0.95
epsilon = 1e-08
bias_one = 1.0 - beta_one**STEP
bias_two = 1.0 - beta_two**STEP

GROUPS = 4
ROWS_VMEM = 58 * 2**20
ROWS_FLOPS = 2**16


def shifted(x, parts, by):
    return lax.ppermute(x, "tensor", [((i + by) % parts, i) for i in range(parts)])


def after_kernel(sent_ref, after_ref, out_ref):
    pass


def list_kernel(list_ref, count_ref, sent_ref):
    slots = list_ref.shape[1]
    place = lax.broadcasted_iota(jnp.int32, sent_ref.shape, 2)
    entry = jnp.where(place == slots, count_ref[0], 0)
    for s in range(slots):
        entry = jnp.where(place == s, list_ref[0, s], entry)
    sent_ref[...] = entry


def pack_kernel(share, after_ref, basis_ref, first_ref, second_ref, to_left_ref, to_right_ref):
    slots, width, _ = basis_ref.shape
    rows = first_ref.shape[1]
    owners = rows // (GROUPS * share)
    me = lax.axis_index("tensor") + GROUPS
    piece = 4 * share * owners

    def put(ref, at, target, s):
        base = lax.rem(target, GROUPS) * share
        for i, source in enumerate((first_ref, second_ref)):
            for r in range(share):
                x = source[s, pl.ds(base + r, owners, stride=GROUPS * share), :]
                high = x.astype(jnp.bfloat16)
                low = (x - high.astype(jnp.float32)).astype(jnp.bfloat16)
                here = at + (2 * i * share + r) * owners
                ref[pl.ds(here, owners), :] = high
                ref[pl.ds(here + share * owners, owners), :] = low

    for ref, far, step in ((to_left_ref, 0, -1), (to_right_ref, 1, 1)):
        ref[pl.ds(0, width), :] = basis_ref[far]
        put(ref, width, me + 2 * step, far)
        ref[pl.ds(width + piece, width), :] = basis_ref[1 - far]
        for s in range(slots):
            put(ref, 2 * width + (1 + s) * piece, me + step, s)


def spread_rows(tiles, spread_ref):
    rows, pieces, part = tiles.shape
    spread_ref[...] = tiles.reshape(rows * pieces, part).astype(jnp.float32)
    return jnp.concatenate(
        [spread_ref[pl.ds(j, rows, stride=pieces), :] for j in range(pieces)], axis=1
    ).astype(jnp.bfloat16)


def toward(turned, first, second):
    moment_one = beta_one * first + (1.0 - beta_one) * turned
    moment_two = beta_two * second + (1.0 - beta_two) * turned * turned
    return moment_one / bias_one / (jnp.sqrt(moment_two / bias_two) + epsilon)


def sent_moments(ref, at, r, share, owners):
    return (
        ref[pl.ds(at + (2 * m * share + r) * owners, owners), :].astype(jnp.float32)
        + ref[pl.ds(at + ((2 * m + 1) * share + r) * owners, owners), :].astype(jnp.float32)
        for m in range(2)
    )


def started(ends, sems):
    copies = [
        [pltpu.make_async_copy(*pair, sems.at[s, i]) for i, pair in enumerate(ends(s))]
        for s in range(sems.shape[0])
    ]
    for copy in sum(copies, []):
        copy.start()
    return copies


def near_rows_kernel(
    share, arrived_hbm, basis_hbm, first_hbm, second_hbm, right_hbm, left_hbm, place_hbm,
    grad_ref, total_ref, rotated_ref, direction_ref, spread_ref, arrived_ref, basis_ref,
    first_ref, second_ref, right_ref, left_ref, sems,
):
    owners, slots, _, pieces, part = arrived_ref.shape
    rows = owners * share
    width = pieces * part
    base = lax.rem(lax.axis_index("tensor"), GROUPS) * share
    piece = 4 * share * owners
    stay = width + piece

    def needed(s):
        near = stay + width + s * piece
        yield arrived_hbm.at[:, s], arrived_ref.at[:, s]
        yield basis_hbm.at[s], basis_ref.at[s]
        for hbm, ref, at in ((right_hbm, right_ref, (0, stay)[s]), (left_hbm, left_ref, (stay, 0)[s])):
            for first, size in ((at, width), (near, piece)):
                yield hbm.at[pl.ds(first, size)], ref.at[pl.ds(first, size)]
        yield first_hbm.at[s], first_ref.at[s]
        yield second_hbm.at[s], second_ref.at[s]

    copies = started(needed, sems)
    for s in range(slots):
        for copy in copies[s]:
            copy.wait()
        near = stay + width + s * piece
        sources = ((right_ref, (0, stay)[s]), (left_ref, (stay, 0)[s]))
        basis = jnp.concatenate(
            [basis_ref[s]] + [ref[pl.ds(at, width), :] for ref, at in sources], axis=1
        )
        grad = spread_rows(arrived_ref[:, s].reshape(rows, pieces, part), spread_ref)
        grad_ref[s] = grad
        rotated = jnp.dot(grad, basis, preferred_element_type=jnp.float32)
        for i in range(GROUPS - 1):
            rotated_ref[s, i] = rotated[:, i * part : (i + 1) * part]
            for r in range(share):
                local = pl.ds(r, owners, stride=share)
                if i == 0:
                    here = pl.ds(base + r, owners, stride=GROUPS * share)
                    first, second = first_ref[s, here, :], second_ref[s, here, :]
                else:
                    first, second = sent_moments(sources[i - 1][0], near, r, share, owners)
                direction_ref[s, i, local, :] = toward(rotated_ref[s, i, local, :], first, second)
        direction = jnp.concatenate([direction_ref[s, i] for i in range(GROUPS - 1)], axis=1)
        total_ref[s] = lax.dot_general(
            direction.astype(jnp.bfloat16),
            basis,
            (((1,), (1,)), ((), ())),
            preferred_element_type=jnp.float32,
        )


def far_rows_kernel(
    share, grad_hbm, total_hbm, far_right_hbm, far_left_hbm, back_ref,
    rotated_ref, direction_ref, spread_ref, grad_ref, total_ref, far_ref, sems,
):
    owners, slots, _, pieces, part = back_ref.shape
    rows = owners * share
    width = pieces * part

    def needed(s):
        yield grad_hbm.at[s], grad_ref.at[s]
        yield (far_right_hbm, far_left_hbm)[s], far_ref.at[s]
        yield total_hbm.at[s], total_ref.at[s]

    copies = started(needed, sems)
    for s in range(slots):
        for copy in copies[s]:
            copy.wait()
        basis = far_ref[s, pl.ds(0, width), :]
        rotated_ref[s] = jnp.dot(grad_ref[s], basis, preferred_element_type=jnp.float32)
        for r in range(share):
            local = pl.ds(r, owners, stride=share)
            first, second = sent_moments(far_ref.at[s], width, r, share, owners)
            direction_ref[s, local, :] = toward(rotated_ref[s, local, :], first, second)
        back = total_ref[s] + lax.dot_general(
            direction_ref[s].astype(jnp.bfloat16),
            basis,
            (((1,), (1,)), ((), ())),
            preferred_element_type=jnp.float32,
        )
        for j in range(pieces):
            spread_ref[pl.ds(j, rows, stride=pieces), :] = back[:, j * part : (j + 1) * part]
        back_ref[:, s] = (
            spread_ref[...].astype(back_ref.dtype).reshape(owners, share, pieces, part)
        )


def near_kernel(
    share, count_ref, grad_ref, right_ref, left_ref, basis_ref, stats_ref, first_ref, second_ref,
    new_stats_ref, new_first_ref, new_second_ref, rotated_ref, spread_ref, all_ref,
):
    owners, slots, _, pieces, part = grad_ref.shape
    rows = owners * share
    me = lax.axis_index("tensor")
    start = pl.multiple_of(me * part, part)
    for s in range(slots):
        live = s < count_ref[0]
        for i, ref in enumerate((grad_ref, right_ref, left_ref)):
            all_ref[s, pl.ds(i * rows, rows), :] = spread_rows(
                ref[:, s].reshape(rows, pieces, part), spread_ref
            )
        grad = all_ref[s]
        grad_cols = all_ref[s, :, pl.ds(start, part)]
        gram = lax.dot_general(
            grad, grad_cols, (((0,), (0,)), ((), ())), preferred_element_type=jnp.float32
        )
        stats = stats_ref[s]
        new_stats_ref[s] = jnp.where(live, beta_stat * stats + (1.0 - beta_stat) * gram, stats)
        rotated_ref[s] = jnp.dot(grad, basis_ref[s], preferred_element_type=jnp.float32)
        for i, offset in enumerate((0, 1, GROUPS - 1)):
            base = lax.rem(me + offset, GROUPS) * share
            for r in range(share):
                rotated = rotated_ref[s, pl.ds(i * rows + r, owners, stride=share), :]
                here = pl.ds(base + r, owners, stride=GROUPS * share)
                first = first_ref[s, here, :]
                second = second_ref[s, here, :]
                new_first_ref[s, here, :] = jnp.where(
                    live, beta_one * first + (1.0 - beta_one) * rotated, first
                )
                new_second_ref[s, here, :] = jnp.where(
                    live, beta_two * second + (1.0 - beta_two) * rotated * rotated, second
                )
        base = lax.rem(me + 2, GROUPS) * share
        for r in range(share):
            here = pl.ds(base + r, owners, stride=GROUPS * share)
            new_first_ref[s, here, :] = first_ref[s, here, :]
            new_second_ref[s, here, :] = second_ref[s, here, :]


def far_kernel(
    share, count_ref, far_ref, basis_ref, stats_ref, first_ref, second_ref,
    new_stats_hbm, new_first_hbm, new_second_hbm,
    new_stats_ref, new_first_ref, new_second_ref, rotated_ref, spread_ref, grad_ref, sems,
):
    owners, slots, _, pieces, part = far_ref.shape
    rows = owners * share
    me = lax.axis_index("tensor")
    start = pl.multiple_of(me * part, part)
    base = lax.rem(me + 2, GROUPS) * share
    copies = []
    for s in range(slots):
        live = s < count_ref[0]
        grad_ref[s] = spread_rows(far_ref[:, s].reshape(rows, pieces, part), spread_ref)
        gram = lax.dot_general(
            grad_ref[s],
            grad_ref[s, :, pl.ds(start, part)],
            (((0,), (0,)), ((), ())),
            preferred_element_type=jnp.float32,
        )
        stats = stats_ref[s]
        new_stats_ref[s] = jnp.where(live, stats + (1.0 - beta_stat) * gram, stats)
        rotated_ref[s] = jnp.dot(grad_ref[s], basis_ref[s], preferred_element_type=jnp.float32)
        new_first_ref[s] = first_ref[s]
        new_second_ref[s] = second_ref[s]
        for r in range(share):
            rotated = rotated_ref[s, pl.ds(r, owners, stride=share), :]
            here = pl.ds(base + r, owners, stride=GROUPS * share)
            first = first_ref[s, here, :]
            second = second_ref[s, here, :]
            new_first_ref[s, here, :] = jnp.where(
                live, beta_one * first + (1.0 - beta_one) * rotated, first
            )
            new_second_ref[s, here, :] = jnp.where(
                live, beta_two * second + (1.0 - beta_two) * rotated * rotated, second
            )
        for i, (ref, hbm) in enumerate((
            (new_stats_ref, new_stats_hbm),
            (new_first_ref, new_first_hbm),
            (new_second_ref, new_second_hbm),
        )):
            copy = pltpu.make_async_copy(ref.at[s], hbm.at[s], sems.at[s, i])
            copy.start()
            copies.append(copy)
    for copy in copies:
        copy.wait()


def add_kernel(partial_ref, update_ref):
    groups, share = GROUPS, partial_ref.shape[2]
    pieces, part = partial_ref.shape[1], partial_ref.shape[3]
    total = partial_ref[:groups].astype(jnp.float32) + partial_ref[groups:].astype(jnp.float32)
    for c in range(pieces):
        update_ref[:, c * part : (c + 1) * part] = (
            total[:, c].reshape(groups * share, part).astype(update_ref.dtype)
        )


def on_device(gradient, block_list, block_counts, stats, basis, first_moment, second_moment):
    rows_dev, cols_dev = gradient.shape
    slot_count = block_list.shape[1]
    owners = lax.axis_size("dp")
    parts = lax.axis_size("tensor")
    width = stats.shape[2]
    part = stats.shape[3]
    blocks = cols_dev * parts // width
    share = rows_dev // GROUPS
    pieces = cols_dev // part
    vmem = pl.BlockSpec(memory_space=pltpu.VMEM)
    smem = pl.BlockSpec(memory_space=pltpu.SMEM)
    params = pltpu.CompilerParams(vmem_limit_bytes=24 * 2**20)

    def own(kernel):
        return lambda *refs: kernel(share, *refs)

    groups = gradient.reshape(GROUPS, share, pieces, part).transpose(0, 2, 1, 3)
    leaving = jnp.tile(groups, (parts // GROUPS, 1, 1, 1))
    moved = lax.all_to_all(leaving, "tensor", 0, 0, tiled=True)
    by_block = moved.reshape(blocks, width // part, share, part).transpose(0, 2, 1, 3)

    mine = pl.pallas_call(
        list_kernel,
        out_shape=jax.ShapeDtypeStruct((owners, 1, part), jnp.int32),
        in_specs=[smem, smem],
        out_specs=vmem,
        compiler_params=params,
        name="list",
    )(block_list, block_counts)
    mine = pl.pallas_call(
        after_kernel,
        out_shape=jax.ShapeDtypeStruct(mine.shape, mine.dtype),
        in_specs=[pl.BlockSpec(memory_space=pl.ANY)] * 2,
        out_specs=pl.BlockSpec(memory_space=pl.ANY),
        input_output_aliases={0: 0},
        name="after",
    )(mine, moved)
    table = lax.all_to_all(mine, "dp", 0, 0, tiled=True).reshape(owners, part)
    lists = table[:, :slot_count]
    live = jnp.arange(slot_count)[None, :] < table[:, slot_count : slot_count + 1]

    piece = 4 * share * owners
    sent = jax.ShapeDtypeStruct((2 * width + 3 * piece, part), jnp.bfloat16)
    packed = pl.pallas_call(
        own(pack_kernel),
        out_shape=(sent, sent),
        in_specs=[pl.BlockSpec(memory_space=pl.ANY)] + [vmem] * 3,
        out_specs=(vmem,) * 2,
        compiler_params=params,
        name="pack",
    )(leaving, basis[0], first_moment[0], second_moment[0])
    right, left = shifted(packed[0], parts, 1), shifted(packed[1], parts, -1)
    far = (shifted(x[: width + piece], parts, by) for x, by in ((right, 1), (left, -1)))

    outgoing = jnp.take(by_block, lists, axis=0, mode="clip")
    arrived = lax.all_to_all(outgoing, "dp", 0, 0, tiled=True)
    holds = (lists.reshape(-1)[None, :] == jnp.arange(blocks)[:, None]) & live.reshape(-1)[None, :]
    place = jnp.argmax(holds, axis=1)
    rows = owners * share
    operands = (arrived, basis[0], first_moment[0], second_moment[0], right, left)
    anywhere = pl.BlockSpec(memory_space=pl.ANY)
    rows_params = pltpu.CompilerParams(vmem_limit_bytes=ROWS_VMEM)
    spread_rows_vmem = pltpu.VMEM((rows * (width // part), part), jnp.float32)
    grad_rows, total = pl.pallas_call(
        own(near_rows_kernel),
        out_shape=(
            jax.ShapeDtypeStruct((slot_count, rows, width), jnp.bfloat16),
            jax.ShapeDtypeStruct((slot_count, rows, width), jnp.float32),
        ),
        in_specs=[anywhere] * (len(operands) + 1),
        out_specs=(vmem,) * 2,
        scratch_shapes=[
            pltpu.VMEM((slot_count, GROUPS - 1, rows, part), jnp.float32),
            pltpu.VMEM((slot_count, GROUPS - 1, rows, part), jnp.float32),
            spread_rows_vmem,
            *(pltpu.VMEM(x.shape, x.dtype) for x in operands),
            pltpu.SemaphoreType.DMA((slot_count, 8)),
        ],
        compiler_params=rows_params,
        cost_estimate=pl.CostEstimate(flops=ROWS_FLOPS, bytes_accessed=2**10, transcendentals=0),
        name="near_rows",
    )(*operands, place)
    far_right, far_left = far
    back = pl.pallas_call(
        own(far_rows_kernel),
        out_shape=jax.ShapeDtypeStruct(arrived.shape, jnp.bfloat16),
        in_specs=[anywhere] * 4,
        out_specs=vmem,
        scratch_shapes=[
            pltpu.VMEM((slot_count, rows, part), jnp.float32),
            pltpu.VMEM((slot_count, rows, part), jnp.float32),
            spread_rows_vmem,
            pltpu.VMEM(grad_rows.shape, grad_rows.dtype),
            pltpu.VMEM(total.shape, total.dtype),
            pltpu.VMEM((slot_count, *far_right.shape), far_right.dtype),
            pltpu.SemaphoreType.DMA((slot_count, 3)),
        ],
        compiler_params=rows_params,
        name="far_rows",
    )(grad_rows, total, far_right, far_left)

    returned = lax.all_to_all(back, "dp", 0, 0, tiled=True)
    placed = jnp.take(
        returned.reshape(owners * slot_count, share, width // part, part), place, axis=0, mode="clip"
    ).transpose(0, 2, 1, 3)
    partial = lax.all_to_all(
        placed.reshape(parts, pieces, share, part), "tensor", 0, 0, tiled=True
    )
    update = pl.pallas_call(
        add_kernel,
        out_shape=jax.ShapeDtypeStruct(gradient.shape, gradient.dtype),
        compiler_params=params,
        name="add",
    )(partial)

    right_rows, left_rows = shifted(arrived, parts, 1), shifted(arrived, parts, -1)
    far_rows = shifted(right_rows, parts, 1)
    states = (stats[0], first_moment[0], second_moment[0])
    shapes = tuple(jax.ShapeDtypeStruct(x.shape, jnp.float32) for x in states)
    spread = pltpu.VMEM((rows * (width // part), part), jnp.float32)
    near = pl.pallas_call(
        own(near_kernel),
        out_shape=shapes,
        in_specs=[smem] + [vmem] * 7,
        out_specs=(vmem,) * 3,
        scratch_shapes=[
            pltpu.VMEM((slot_count, 3 * rows, part), jnp.float32),
            spread,
            pltpu.VMEM((slot_count, 3 * rows, width), jnp.bfloat16),
        ],
        compiler_params=params,
        cost_estimate=pl.CostEstimate(flops=2**32, bytes_accessed=2**24, transcendentals=0),
        name="near_state",
    )(block_counts, arrived, right_rows, left_rows, basis[0], *states)
    new_stats, new_first, new_second = pl.pallas_call(
        own(far_kernel),
        out_shape=shapes,
        in_specs=[smem] + [vmem] * 5,
        out_specs=(pl.BlockSpec(memory_space=pl.ANY),) * 3,
        scratch_shapes=[
            *(pltpu.VMEM(x.shape, x.dtype) for x in shapes),
            pltpu.VMEM((slot_count, rows, part), jnp.float32),
            spread,
            pltpu.VMEM((slot_count, rows, width), jnp.bfloat16),
            pltpu.SemaphoreType.DMA((slot_count, 3)),
        ],
        compiler_params=params,
        name="far_state",
    )(block_counts, far_rows, basis[0], *near)
    return (update, new_stats[None], new_first[None], new_second[None])


def solution(mesh):
    placed = (
        P("dp", "tensor"),
        P("dp", None),
        P("dp"),
        P("dp", None, None, "tensor"),
        P("dp", None, None, "tensor"),
        P("dp", None, None, "tensor"),
        P("dp", None, None, "tensor"),
    )
    return jax.shard_map(
        on_device,
        mesh=mesh,
        in_specs=placed,
        out_specs=(
            P("dp", "tensor"),
            P("dp", None, None, "tensor"),
            P("dp", None, None, "tensor"),
            P("dp", None, None, "tensor"),
        ),
        check_vma=False,
    )
```

```python
import jax
import jax.numpy as jnp
from jax import lax
from jax.experimental import pallas as pl
from jax.experimental.pallas import tpu as pltpu
from jax.sharding import PartitionSpec as P

STEP = 10


beta_one = 0.9
beta_two = 0.95
beta_stat = 0.95
epsilon = 1e-08
bias_one = 1.0 - beta_one**STEP
bias_two = 1.0 - beta_two**STEP

GROUPS = 4
ROWS_VMEM = 58 * 2**20
ROWS_FLOPS = 2**16


def shifted(x, parts, by):
    return lax.ppermute(x, "tensor", [((i + by) % parts, i) for i in range(parts)])


def after_kernel(sent_ref, after_ref, out_ref):
    pass


def list_kernel(list_ref, count_ref, sent_ref):
    slots = list_ref.shape[1]
    place = lax.broadcasted_iota(jnp.int32, sent_ref.shape, 2)
    entry = jnp.where(place == slots, count_ref[0], 0)
    for s in range(slots):
        entry = jnp.where(place == s, list_ref[0, s], entry)
    sent_ref[...] = entry


def pack_kernel(share, after_ref, basis_ref, first_ref, second_ref, to_left_ref, to_right_ref):
    slots, width, _ = basis_ref.shape
    rows = first_ref.shape[1]
    owners = rows // (GROUPS * share)
    me = lax.axis_index("tensor") + GROUPS
    piece = 4 * share * owners

    def put(ref, at, target, s):
        base = lax.rem(target, GROUPS) * share
        for i, source in enumerate((first_ref, second_ref)):
            for r in range(share):
                x = source[s, pl.ds(base + r, owners, stride=GROUPS * share), :]
                high = x.astype(jnp.bfloat16)
                low = (x - high.astype(jnp.float32)).astype(jnp.bfloat16)
                here = at + (2 * i * share + r) * owners
                ref[pl.ds(here, owners), :] = high
                ref[pl.ds(here + share * owners, owners), :] = low

    for ref, far, step in ((to_left_ref, 0, -1), (to_right_ref, 1, 1)):
        ref[pl.ds(0, width), :] = basis_ref[far]
        put(ref, width, me + 2 * step, far)
        ref[pl.ds(width + piece, width), :] = basis_ref[1 - far]
        for s in range(slots):
            put(ref, 2 * width + (1 + s) * piece, me + step, s)


def spread_rows(tiles, spread_ref):
    rows, pieces, part = tiles.shape
    spread_ref[...] = tiles.reshape(rows * pieces, part).astype(jnp.float32)
    return jnp.concatenate(
        [spread_ref[pl.ds(j, rows, stride=pieces), :] for j in range(pieces)], axis=1
    ).astype(jnp.bfloat16)


def toward(turned, first, second):
    moment_one = beta_one * first + (1.0 - beta_one) * turned
    moment_two = beta_two * second + (1.0 - beta_two) * turned * turned
    return moment_one / bias_one / (jnp.sqrt(moment_two / bias_two) + epsilon)


def sent_moments(ref, at, r, share, owners):
    return (
        ref[pl.ds(at + (2 * m * share + r) * owners, owners), :].astype(jnp.float32)
        + ref[pl.ds(at + ((2 * m + 1) * share + r) * owners, owners), :].astype(jnp.float32)
        for m in range(2)
    )


def started(ends, sems):
    copies = [
        [pltpu.make_async_copy(*pair, sems.at[s, i]) for i, pair in enumerate(ends(s))]
        for s in range(sems.shape[0])
    ]
    for copy in sum(copies, []):
        copy.start()
    return copies


def near_rows_kernel(
    share, arrived_hbm, basis_hbm, first_hbm, second_hbm, right_hbm, left_hbm, place_hbm,
    grad_ref, total_ref, rotated_ref, direction_ref, spread_ref, arrived_ref, basis_ref,
    first_ref, second_ref, right_ref, left_ref, sems,
):
    owners, slots, _, pieces, part = arrived_ref.shape
    rows = owners * share
    width = pieces * part
    base = lax.rem(lax.axis_index("tensor"), GROUPS) * share
    piece = 4 * share * owners
    stay = width + piece

    def needed(s):
        near = stay + width + s * piece
        yield arrived_hbm.at[:, s], arrived_ref.at[:, s]
        yield basis_hbm.at[s], basis_ref.at[s]
        for hbm, ref, at in ((right_hbm, right_ref, (0, stay)[s]), (left_hbm, left_ref, (stay, 0)[s])):
            for first, size in ((at, width), (near, piece)):
                yield hbm.at[pl.ds(first, size)], ref.at[pl.ds(first, size)]
        yield first_hbm.at[s], first_ref.at[s]
        yield second_hbm.at[s], second_ref.at[s]

    copies = started(needed, sems)
    for s in range(slots):
        for copy in copies[s]:
            copy.wait()
        near = stay + width + s * piece
        sources = ((right_ref, (0, stay)[s]), (left_ref, (stay, 0)[s]))
        basis = jnp.concatenate(
            [basis_ref[s]] + [ref[pl.ds(at, width), :] for ref, at in sources], axis=1
        )
        grad = spread_rows(arrived_ref[:, s].reshape(rows, pieces, part), spread_ref)
        grad_ref[s] = grad
        rotated = jnp.dot(grad, basis, preferred_element_type=jnp.float32)
        for i in range(GROUPS - 1):
            rotated_ref[s, i] = rotated[:, i * part : (i + 1) * part]
            for r in range(share):
                local = pl.ds(r, owners, stride=share)
                if i == 0:
                    here = pl.ds(base + r, owners, stride=GROUPS * share)
                    first, second = first_ref[s, here, :], second_ref[s, here, :]
                else:
                    first, second = sent_moments(sources[i - 1][0], near, r, share, owners)
                direction_ref[s, i, local, :] = toward(rotated_ref[s, i, local, :], first, second)
        direction = jnp.concatenate([direction_ref[s, i] for i in range(GROUPS - 1)], axis=1)
        total_ref[s] = lax.dot_general(
            direction.astype(jnp.bfloat16),
            basis,
            (((1,), (1,)), ((), ())),
            preferred_element_type=jnp.float32,
        )


def far_rows_kernel(
    share, grad_hbm, total_hbm, far_right_hbm, far_left_hbm, back_ref,
    rotated_ref, direction_ref, spread_ref, grad_ref, total_ref, far_ref, sems,
):
    owners, slots, _, pieces, part = back_ref.shape
    rows = owners * share
    width = pieces * part

    def needed(s):
        yield grad_hbm.at[s], grad_ref.at[s]
        yield (far_right_hbm, far_left_hbm)[s], far_ref.at[s]
        yield total_hbm.at[s], total_ref.at[s]

    copies = started(needed, sems)
    for s in range(slots):
        for copy in copies[s]:
            copy.wait()
        basis = far_ref[s, pl.ds(0, width), :]
        rotated_ref[s] = jnp.dot(grad_ref[s], basis, preferred_element_type=jnp.float32)
        for r in range(share):
            local = pl.ds(r, owners, stride=share)
            first, second = sent_moments(far_ref.at[s], width, r, share, owners)
            direction_ref[s, local, :] = toward(rotated_ref[s, local, :], first, second)
        back = total_ref[s] + lax.dot_general(
            direction_ref[s].astype(jnp.bfloat16),
            basis,
            (((1,), (1,)), ((), ())),
            preferred_element_type=jnp.float32,
        )
        for j in range(pieces):
            spread_ref[pl.ds(j, rows, stride=pieces), :] = back[:, j * part : (j + 1) * part]
        back_ref[:, s] = (
            spread_ref[...].astype(back_ref.dtype).reshape(owners, share, pieces, part)
        )


def near_kernel(
    share, count_ref, grad_ref, right_ref, left_ref, basis_ref, stats_ref, first_ref, second_ref,
    new_stats_ref, new_first_ref, new_second_ref, rotated_ref, spread_ref, all_ref,
):
    owners, slots, _, pieces, part = grad_ref.shape
    rows = owners * share
    me = lax.axis_index("tensor")
    start = pl.multiple_of(me * part, part)
    for s in range(slots):
        live = s < count_ref[0]
        for i, ref in enumerate((grad_ref, right_ref, left_ref)):
            all_ref[s, pl.ds(i * rows, rows), :] = spread_rows(
                ref[:, s].reshape(rows, pieces, part), spread_ref
            )
        grad = all_ref[s]
        grad_cols = all_ref[s, :, pl.ds(start, part)]
        gram = lax.dot_general(
            grad, grad_cols, (((0,), (0,)), ((), ())), preferred_element_type=jnp.float32
        )
        stats = stats_ref[s]
        new_stats_ref[s] = jnp.where(live, beta_stat * stats + (1.0 - beta_stat) * gram, stats)
        rotated_ref[s] = jnp.dot(grad, basis_ref[s], preferred_element_type=jnp.float32)
        for i, offset in enumerate((0, 1, GROUPS - 1)):
            base = lax.rem(me + offset, GROUPS) * share
            for r in range(share):
                rotated = rotated_ref[s, pl.ds(i * rows + r, owners, stride=share), :]
                here = pl.ds(base + r, owners, stride=GROUPS * share)
                first = first_ref[s, here, :]
                second = second_ref[s, here, :]
                new_first_ref[s, here, :] = jnp.where(
                    live, beta_one * first + (1.0 - beta_one) * rotated, first
                )
                new_second_ref[s, here, :] = jnp.where(
                    live, beta_two * second + (1.0 - beta_two) * rotated * rotated, second
                )
        base = lax.rem(me + 2, GROUPS) * share
        for r in range(share):
            here = pl.ds(base + r, owners, stride=GROUPS * share)
            new_first_ref[s, here, :] = first_ref[s, here, :]
            new_second_ref[s, here, :] = second_ref[s, here, :]


def far_kernel(
    share, count_ref, far_ref, basis_ref, stats_ref, first_ref, second_ref,
    new_stats_hbm, new_first_hbm, new_second_hbm,
    new_stats_ref, new_first_ref, new_second_ref, rotated_ref, spread_ref, grad_ref, sems,
):
    owners, slots, _, pieces, part = far_ref.shape
    rows = owners * share
    me = lax.axis_index("tensor")
    start = pl.multiple_of(me * part, part)
    base = lax.rem(me + 2, GROUPS) * share
    copies = []
    for s in range(slots):
        live = s < count_ref[0]
        grad_ref[s] = spread_rows(far_ref[:, s].reshape(rows, pieces, part), spread_ref)
        gram = lax.dot_general(
            grad_ref[s],
            grad_ref[s, :, pl.ds(start, part)],
            (((0,), (0,)), ((), ())),
            preferred_element_type=jnp.float32,
        )
        stats = stats_ref[s]
        new_stats_ref[s] = jnp.where(live, stats + (1.0 - beta_stat) * gram, stats)
        rotated_ref[s] = jnp.dot(grad_ref[s], basis_ref[s], preferred_element_type=jnp.float32)
        new_first_ref[s] = first_ref[s]
        new_second_ref[s] = second_ref[s]
        for r in range(share):
            rotated = rotated_ref[s, pl.ds(r, owners, stride=share), :]
            here = pl.ds(base + r, owners, stride=GROUPS * share)
            first = first_ref[s, here, :]
            second = second_ref[s, here, :]
            new_first_ref[s, here, :] = jnp.where(
                live, beta_one * first + (1.0 - beta_one) * rotated, first
            )
            new_second_ref[s, here, :] = jnp.where(
                live, beta_two * second + (1.0 - beta_two) * rotated * rotated, second
            )
        for i, (ref, hbm) in enumerate((
            (new_stats_ref, new_stats_hbm),
            (new_first_ref, new_first_hbm),
            (new_second_ref, new_second_hbm),
        )):
            copy = pltpu.make_async_copy(ref.at[s], hbm.at[s], sems.at[s, i])
            copy.start()
            copies.append(copy)
    for copy in copies:
        copy.wait()


def add_kernel(partial_ref, update_ref):
    groups, share = GROUPS, partial_ref.shape[2]
    pieces, part = partial_ref.shape[1], partial_ref.shape[3]
    total = partial_ref[:groups].astype(jnp.float32) + partial_ref[groups:].astype(jnp.float32)
    for c in range(pieces):
        update_ref[:, c * part : (c + 1) * part] = (
            total[:, c].reshape(groups * share, part).astype(update_ref.dtype)
        )


def on_device(gradient, block_list, block_counts, stats, basis, first_moment, second_moment):
    rows_dev, cols_dev = gradient.shape
    slot_count = block_list.shape[1]
    owners = lax.axis_size("dp")
    parts = lax.axis_size("tensor")
    width = stats.shape[2]
    part = stats.shape[3]
    blocks = cols_dev * parts // width
    share = rows_dev // GROUPS
    pieces = cols_dev // part
    vmem = pl.BlockSpec(memory_space=pltpu.VMEM)
    smem = pl.BlockSpec(memory_space=pltpu.SMEM)
    params = pltpu.CompilerParams(vmem_limit_bytes=24 * 2**20)

    def own(kernel):
        return lambda *refs: kernel(share, *refs)

    groups = gradient.reshape(GROUPS, share, pieces, part).transpose(0, 2, 1, 3)
    leaving = jnp.tile(groups, (parts // GROUPS, 1, 1, 1))
    moved = lax.all_to_all(leaving, "tensor", 0, 0, tiled=True)
    by_block = moved.reshape(blocks, width // part, share, part).transpose(0, 2, 1, 3)

    mine = pl.pallas_call(
        list_kernel,
        out_shape=jax.ShapeDtypeStruct((owners, 1, part), jnp.int32),
        in_specs=[smem, smem],
        out_specs=vmem,
        compiler_params=params,
        name="list",
    )(block_list, block_counts)
    mine = pl.pallas_call(
        after_kernel,
        out_shape=jax.ShapeDtypeStruct(mine.shape, mine.dtype),
        in_specs=[pl.BlockSpec(memory_space=pl.ANY)] * 2,
        out_specs=pl.BlockSpec(memory_space=pl.ANY),
        input_output_aliases={0: 0},
        name="after",
    )(mine, moved)
    table = lax.all_to_all(mine, "dp", 0, 0, tiled=True).reshape(owners, part)
    lists = table[:, :slot_count]
    live = jnp.arange(slot_count)[None, :] < table[:, slot_count : slot_count + 1]

    piece = 4 * share * owners
    sent = jax.ShapeDtypeStruct((2 * width + 3 * piece, part), jnp.bfloat16)
    packed = pl.pallas_call(
        own(pack_kernel),
        out_shape=(sent, sent),
        in_specs=[pl.BlockSpec(memory_space=pl.ANY)] + [vmem] * 3,
        out_specs=(vmem,) * 2,
        compiler_params=params,
        name="pack",
    )(leaving, basis[0], first_moment[0], second_moment[0])
    right, left = shifted(packed[0], parts, 1), shifted(packed[1], parts, -1)
    far = (shifted(x[: width + piece], parts, by) for x, by in ((right, 1), (left, -1)))

    outgoing = jnp.take(by_block, lists, axis=0, mode="clip")
    arrived = lax.all_to_all(outgoing, "dp", 0, 0, tiled=True)
    holds = (lists.reshape(-1)[None, :] == jnp.arange(blocks)[:, None]) & live.reshape(-1)[None, :]
    place = jnp.argmax(holds, axis=1)
    rows = owners * share
    operands = (arrived, basis[0], first_moment[0], second_moment[0], right, left)
    anywhere = pl.BlockSpec(memory_space=pl.ANY)
    rows_params = pltpu.CompilerParams(vmem_limit_bytes=ROWS_VMEM)
    spread_rows_vmem = pltpu.VMEM((rows * (width // part), part), jnp.float32)
    grad_rows, total = pl.pallas_call(
        own(near_rows_kernel),
        out_shape=(
            jax.ShapeDtypeStruct((slot_count, rows, width), jnp.bfloat16),
            jax.ShapeDtypeStruct((slot_count, rows, width), jnp.float32),
        ),
        in_specs=[anywhere] * (len(operands) + 1),
        out_specs=(vmem,) * 2,
        scratch_shapes=[
            pltpu.VMEM((slot_count, GROUPS - 1, rows, part), jnp.float32),
            pltpu.VMEM((slot_count, GROUPS - 1, rows, part), jnp.float32),
            spread_rows_vmem,
            *(pltpu.VMEM(x.shape, x.dtype) for x in operands),
            pltpu.SemaphoreType.DMA((slot_count, 8)),
        ],
        compiler_params=rows_params,
        cost_estimate=pl.CostEstimate(flops=ROWS_FLOPS, bytes_accessed=2**10, transcendentals=0),
        name="near_rows",
    )(*operands, place)
    far_right, far_left = far
    back = pl.pallas_call(
        own(far_rows_kernel),
        out_shape=jax.ShapeDtypeStruct(arrived.shape, jnp.bfloat16),
        in_specs=[anywhere] * 4,
        out_specs=vmem,
        scratch_shapes=[
            pltpu.VMEM((slot_count, rows, part), jnp.float32),
            pltpu.VMEM((slot_count, rows, part), jnp.float32),
            spread_rows_vmem,
            pltpu.VMEM(grad_rows.shape, grad_rows.dtype),
            pltpu.VMEM(total.shape, total.dtype),
            pltpu.VMEM((slot_count, *far_right.shape), far_right.dtype),
            pltpu.SemaphoreType.DMA((slot_count, 3)),
        ],
        compiler_params=params,
        name="far_rows",
    )(grad_rows, total, far_right, far_left)

    returned = lax.all_to_all(back, "dp", 0, 0, tiled=True)
    placed = jnp.take(
        returned.reshape(owners * slot_count, share, width // part, part), place, axis=0, mode="clip"
    ).transpose(0, 2, 1, 3)
    partial = lax.all_to_all(
        placed.reshape(parts, pieces, share, part), "tensor", 0, 0, tiled=True
    )
    update = pl.pallas_call(
        add_kernel,
        out_shape=jax.ShapeDtypeStruct(gradient.shape, gradient.dtype),
        compiler_params=params,
        name="add",
    )(partial)

    right_rows, left_rows = shifted(arrived, parts, 1), shifted(arrived, parts, -1)
    far_rows = shifted(right_rows, parts, 1)
    states = (stats[0], first_moment[0], second_moment[0])
    shapes = tuple(jax.ShapeDtypeStruct(x.shape, jnp.float32) for x in states)
    spread = pltpu.VMEM((rows * (width // part), part), jnp.float32)
    near = pl.pallas_call(
        own(near_kernel),
        out_shape=shapes,
        in_specs=[smem] + [vmem] * 7,
        out_specs=(vmem,) * 3,
        scratch_shapes=[
            pltpu.VMEM((slot_count, 3 * rows, part), jnp.float32),
            spread,
            pltpu.VMEM((slot_count, 3 * rows, width), jnp.bfloat16),
        ],
        compiler_params=params,
        cost_estimate=pl.CostEstimate(flops=2**32, bytes_accessed=2**24, transcendentals=0),
        name="near_state",
    )(block_counts, arrived, right_rows, left_rows, basis[0], *states)
    new_stats, new_first, new_second = pl.pallas_call(
        own(far_kernel),
        out_shape=shapes,
        in_specs=[smem] + [vmem] * 5,
        out_specs=(pl.BlockSpec(memory_space=pl.ANY),) * 3,
        scratch_shapes=[
            *(pltpu.VMEM(x.shape, x.dtype) for x in shapes),
            pltpu.VMEM((slot_count, rows, part), jnp.float32),
            spread,
            pltpu.VMEM((slot_count, rows, width), jnp.bfloat16),
            pltpu.SemaphoreType.DMA((slot_count, 3)),
        ],
        compiler_params=params,
        name="far_state",
    )(block_counts, far_rows, basis[0], *near)
    return (update, new_stats[None], new_first[None], new_second[None])


def solution(mesh):
    placed = (
        P("dp", "tensor"),
        P("dp", None),
        P("dp"),
        P("dp", None, None, "tensor"),
        P("dp", None, None, "tensor"),
        P("dp", None, None, "tensor"),
        P("dp", None, None, "tensor"),
    )
    return jax.shard_map(
        on_device,
        mesh=mesh,
        in_specs=placed,
        out_specs=(
            P("dp", "tensor"),
            P("dp", None, None, "tensor"),
            P("dp", None, None, "tensor"),
            P("dp", None, None, "tensor"),
        ),
        check_vma=False,
    )
```
